256 devices in a mesh: rep: 4 (over y_lo, core), dp: 64 (over x, y_hi, z).
Axes of the slice: x: 4, y: 4 (y_hi: 2, y_lo: 2; y = y_hi * 2 + y_lo), z: 8, core: 2. Of those that a mesh axis runs over, the one named last changes fastest.
Arguments:
- tokens: bfloat16 [32768, 80], P(('rep', 'dp')), may hold values from -6 to 6
- upstream: bfloat16 [32768, 80], P(('rep', 'dp')), may hold values from -6 to 6
- gate_pre: bfloat16 [32768, 14336], P(('rep', 'dp')), may hold values from -6 to 6
- up_pre: bfloat16 [32768, 14336], P(('rep', 'dp')), may hold values from -6 to 6
- param_shards: bfloat16 [34816, 128], P('dp'), may hold values from -0.625 to 0.625
- shard_rows: int32 [64], replicated, may hold values from 316 to 524, as said below
- row_state: float32 [240], replicated, may hold values from 1e-07 to 1e-05
- col_state: float32 [43008], replicated, may hold values from 1e-07 to 1e-05
Outputs:
- new_params: bfloat16 [34816, 128], P('dp')
- direction: bfloat16 [34816, 128], P('dp')
- new_rows: float32 [240], replicated
- new_cols: float32 [43008], replicated
The draws below stay inside these ranges and needn't reach their ends.
Inputs may be any that keep to these rules, and one draw needn't show every extreme that they name: `shard_rows`: owner lengths of the flat buffer in order, summing to 26880; for every p below 64 - 1 the end of owner p lies within 52 rows of (p + 1) * 420; one owner holds exactly 524 rows.
All inputs are finite; a program needn't handle non-finite values.
Results may differ from the reference program's by a relative error of at most 0.0049.
Values may be sent and summed in bfloat16 or wider, within the bound.
A program may use at most 128 MiB of HBM per device.

```python
import math
import jax
import jax.numpy as jnp
from jax import lax

FF = 14336
RB = 80
TOKENS = 32768
ROWS_FLAT = 26880
EV = 420
JIT = 52
CAP = 544
N_DP = 64


def draw_shard_rows(key, part):
    key = jax.random.fold_in(key, 5)
    key_jitter, key_widest = jax.random.split(key)
    inner = jnp.arange(N_DP - 1, dtype=jnp.int32)
    jitter = jax.random.randint(key_jitter, (N_DP - 1,), -JIT, JIT + 1, dtype=jnp.int32)
    widest = jax.random.randint(key_widest, (), 1, N_DP - 1, dtype=jnp.int32)
    jitter = jnp.where(inner == widest, JIT, jnp.where(inner == widest - 1, -JIT, jitter)).astype(jnp.int32)
    inner_ends = ((inner + 1) * EV + jitter).astype(jnp.int32)
    ends = jnp.concatenate([inner_ends, jnp.full((1,), ROWS_FLAT, jnp.int32)])
    begins = jnp.concatenate([jnp.zeros((1,), jnp.int32), inner_ends])
    return (ends - begins).astype(jnp.int32)


def level_of(rng, dims, cuts, smallest, high):
    level, own = 1.0, jax.random.fold_in(rng, 6)
    for dim, shards_of in cuts:
        heights = jnp.exp(jax.random.uniform(jax.random.fold_in(own, dim), (shards_of,), jnp.float32, smallest / len(cuts), high / len(cuts)))
        level = level * jnp.repeat(heights, dims[dim] // shards_of).reshape([-1 if axis == dim else 1 for axis in range(len(dims))])
    return level


def noise(stream_key, extent, deviation, limit, cuts=(), kind=jnp.bfloat16):
    drawn = jax.random.normal(stream_key, extent, jnp.float32) * deviation
    if len(cuts) > 0:
        drawn = level_of(stream_key, extent, cuts, -0.22, 0.18) * drawn
    return jnp.clip(drawn, min=-limit, max=limit).astype(kind)


def setup_inputs(seed: int = 0) -> dict:
    key_of = jax.random.split(jax.random.key(seed), 9)
    tokens = noise(key_of[0], (TOKENS, RB), 1.0, 6.0, ((0, 256),))
    upstream = noise(key_of[1], (TOKENS, RB), 1.0, 6.0, ((0, 256),))
    gate_pre = noise(key_of[2], (TOKENS, FF), 1.0, 6.0, ((0, 256),))
    up_pre = noise(key_of[3], (TOKENS, FF), 1.0, 6.0, ((0, 256),))
    param_shards = noise(key_of[4], (N_DP * CAP, 128), RB ** -0.5, 0.625, ((0, 64),))
    shard_rows = draw_shard_rows(jax.random.fold_in(key_of[8], 71), 0)
    row_state = jnp.clip(jnp.exp(jax.random.uniform(key_of[6], (3 * RB,), jnp.float32, math.log(1.0000000116860974e-07), math.log(9.999999747378752e-06))), 1.0000000116860974e-07, 9.999999747378752e-06)
    col_state = jnp.clip(jnp.exp(jax.random.uniform(key_of[7], (3 * FF,), jnp.float32, math.log(1.0000000116860974e-07), math.log(9.999999747378752e-06))), 1.0000000116860974e-07, 9.999999747378752e-06)
    return {"tokens": tokens, "upstream": upstream, "gate_pre": gate_pre, "up_pre": up_pre, "param_shards": param_shards, "shard_rows": shard_rows, "row_state": row_state, "col_state": col_state}


BETA = 0.8
RHO = 0.2
TINY = 1e-30

def contract_rows(left, right):
    return lax.dot_general(left, right, (((0,), (0,)), ((), ())), preferred_element_type=jnp.float32)

def reference(tokens, upstream, gate_pre, up_pre, param_shards, shard_rows, row_state, col_state):
    per_matrix = RB * FF // 128
    ends = jnp.cumsum(shard_rows).astype(jnp.int32)
    starts = (ends - shard_rows).astype(jnp.int32)
    all_rows = jnp.arange(ROWS_FLAT, dtype=jnp.int32)
    owners = lax.optimization_barrier(jnp.sum((ends[None, :] <= all_rows[:, None]).astype(jnp.int32), axis=1))
    positions = (owners * CAP + all_rows - jnp.take(starts, owners)).astype(jnp.int32)
    flat_weights = jnp.take(param_shards, positions, axis=0)
    w_down = flat_weights[2 * per_matrix:].reshape(RB, FF)
    gate_in = gate_pre.astype(jnp.float32)
    up_in = up_pre.astype(jnp.float32)
    sigmoid_gate = jax.nn.sigmoid(gate_in)
    activated = gate_in * sigmoid_gate
    hidden = (activated * up_in).astype(jnp.bfloat16)
    grad_down = contract_rows(upstream, hidden) / float(TOKENS)
    d_hidden = jnp.dot(upstream, w_down, preferred_element_type=jnp.float32)
    d_gate = (d_hidden * up_in * sigmoid_gate * (1.0 + gate_in * (1.0 - sigmoid_gate))).astype(jnp.bfloat16)
    d_up = (d_hidden * activated).astype(jnp.bfloat16)
    grad_gate = contract_rows(tokens, d_gate) / float(TOKENS)
    grad_up = contract_rows(tokens, d_up) / float(TOKENS)
    grads = [grad_gate, grad_up, grad_down]
    row_total = jnp.concatenate([lax.optimization_barrier(jnp.sum(grad * grad, axis=1)) for grad in grads])
    col_total = jnp.concatenate([lax.optimization_barrier(jnp.sum(grad * grad, axis=0)) for grad in grads])
    new_rows = BETA * row_state + (1.0 - BETA) * (row_total / float(FF) + TINY)
    new_cols = BETA * col_state + (1.0 - BETA) * (col_total / float(RB) + TINY)
    updated_list = []
    direction_list = []
    for number in range(3):
        matrix = flat_weights[number * per_matrix:(number + 1) * per_matrix].astype(jnp.float32).reshape(RB, FF)
        row_part = new_rows[number * RB:(number + 1) * RB]
        col_part = new_cols[number * FF:(number + 1) * FF]
        rows_now = row_part / jnp.mean(row_part)
        moved = grads[number] * lax.rsqrt(rows_now[:, None] * col_part[None, :])
        scale = jnp.sqrt(jnp.mean(matrix * matrix))
        updated_list.append((matrix - RHO * scale * moved).reshape(-1, 128))
        direction_list.append(moved.reshape(-1, 128))
    updated = jnp.concatenate(updated_list, axis=0)
    moves = jnp.concatenate(direction_list, axis=0)
    offsets = jnp.arange(CAP, dtype=jnp.int32)
    indices = jnp.minimum(starts[:, None] + offsets[None, :], ROWS_FLAT - 1).astype(jnp.int32).reshape(-1)
    live_rows = (offsets[None, :] < shard_rows[:, None]).reshape(-1)
    new_params = jnp.where(live_rows[:, None], jnp.take(updated, indices, axis=0), 0.0).astype(jnp.bfloat16)
    direction = jnp.where(live_rows[:, None], jnp.take(moves, indices, axis=0), 0.0).astype(jnp.bfloat16)
    return (new_params, direction, new_rows, new_cols)
```

```python
import functools

import jax
import jax.numpy as jnp
from jax import lax
from jax.experimental import pallas as pl
from jax.experimental.pallas import tpu as pltpu
from jax.sharding import PartitionSpec as P

BETA = 0.8
RHO = 0.2
TINY = 1e-30
RB = 80
NB = 112
EV = 420
JIT = 52
WIN = 528
FIRST = 42
NWIN = 22
PIECES = 7
SLOTS = 256
WPAD = 336
WROWS = 9360
F32 = jnp.float32
BF16 = jnp.bfloat16
VMEM_LIMIT = 56 * 1024 * 1024


def slot_row(pos):
    zz = pos % 4
    second = pos // 4 % 4
    first = pos // 16 % 4
    h = pos // 64 % 2
    core = pos // 128
    z = 2 * zz + h
    x, y = (first, second) if h == 0 else (second, first)
    p = (x * 2 + y // 2) * 8 + z
    r = (y % 2) * 2 + core
    q = (p % 4) * 4 + r
    return None if q == 15 else 15 * (p // 4) + q


def coords():
    r = lax.axis_index("rep")
    p = lax.axis_index("dp")
    x = p // 16
    y = (p // 8 % 2) * 2 + r // 2
    return x, y, p % 8, r % 2


def device(x, y, z, core):
    return {"rep": (y % 2) * 2 + core, "dp": (x * 2 + y // 2) * 8 + z}


def grads_kernel(tok_t, up_t, up, wwin, gate, upp, out, wflat, rows):
    c = pl.program_id(0)

    @pl.when(c == 0)
    def _():
        wflat[...] = jnp.zeros_like(wflat)
        for n in range(NWIN):
            off = EV * (FIRST + n) - JIT - 17920 + WPAD
            wflat[pl.ds(off, WIN), :] += wwin[n].astype(F32)

    def block(jj, carry):
        cols = pl.ds(pl.multiple_of(jj * 256, 256), 256)
        g = gate[:, cols].astype(F32)
        u = upp[:, cols].astype(F32)
        s = 0.5 * jnp.tanh(0.5 * g) + 0.5
        act = g * s
        hid = (act * u).astype(BF16)
        gd = jnp.dot(up_t[...], hid, preferred_element_type=F32)
        j = c * 16 + jj * 2
        w = jnp.concatenate(
            [wflat[pl.ds(WPAD + j + b, RB, stride=NB), :] for b in range(2)], axis=1
        ).astype(BF16)
        dh = jnp.dot(up[...], w, preferred_element_type=F32)
        dg = (dh * u * s * (1.0 + g * (1.0 - s))).astype(BF16)
        du = (dh * act).astype(BF16)
        gg = jnp.dot(tok_t[...], dg, preferred_element_type=F32)
        gu = jnp.dot(tok_t[...], du, preferred_element_type=F32)
        for m, v in enumerate((gg, gu, gd)):
            for b in range(2):
                rows[pl.ds(m * RB * 16 + jj * 2 + b, RB, stride=16), :] = v[:, b * 128 : b * 128 + 128]
        return carry

    lax.fori_loop(0, 8, block, 0)
    for pos in range(SLOTS):
        row = slot_row(pos)
        if row is None:
            out[0, pos] = jnp.zeros((16, 128), BF16)
        else:
            out[0, pos] = rows[row * 16 : row * 16 + 16, :].astype(BF16)


def grads(tokens, upstream, gate_pre, up_pre, wwin):
    whole = lambda shape: pl.BlockSpec(shape, lambda c: (0,) * len(shape))
    return pl.pallas_call(
        grads_kernel,
        grid=(PIECES,),
        in_specs=[
            whole((RB, 128)),
            whole((RB, 128)),
            whole((128, RB)),
            whole((NWIN, WIN, 128)),
            pl.BlockSpec((128, 2048), lambda c: (0, c)),
            pl.BlockSpec((128, 2048), lambda c: (0, c)),
        ],
        out_specs=pl.BlockSpec((1, SLOTS, 16, 128), lambda c: (c, 0, 0, 0)),
        out_shape=jax.ShapeDtypeStruct((PIECES, SLOTS, 16, 128), BF16),
        scratch_shapes=[pltpu.VMEM((WROWS, 128), F32), pltpu.VMEM((240 * 16, 128), F32)],
        compiler_params=pltpu.CompilerParams(vmem_limit_bytes=VMEM_LIMIT),
        name="grads",
    )(tokens.T, upstream.T, upstream, wwin, gate_pre, up_pre)


def greet(targets):
    barrier = pltpu.get_barrier_semaphore()
    for target in targets:
        pl.semaphore_signal(barrier, inc=1, device_id=target, device_id_type=pl.DeviceIdType.MESH)
    pl.semaphore_wait(barrier, len(targets))


def remote(src, dst, send, recv, target):
    return pltpu.make_async_remote_copy(
        src_ref=src, dst_ref=dst, send_sem=send, recv_sem=recv,
        device_id=target, device_id_type=pl.DeviceIdType.MESH,
    )


def scatter_kernel(f, out, c1, a1, c2, a2, a2own, c3, a3, c4, ss1, rs1, ss2, rs2, ss3, rs3, ss4, rs4):
    x, y, z, core = coords()
    axis_of = lambda h: (lambda d: device((x + d) % 4, y, z, core)) if h == 0 else (
        lambda d: device(x, (y + d) % 4, z, core))
    place = (x, y)
    greet(
        [device(x, y, z, 1 - core)]
        + [axis_of(h)(d) for h in range(2) for d in (1, 2, 3)]
        + [device(x, y, (z + d) % 8, core) for d in range(1, 8)]
    )

    def copy1(c):
        return remote(f.at[c, 1 - core], c1.at[c], ss1.at[c], rs1.at[c], device(x, y, z, 1 - core))

    def copy2(c, h, d):
        k = h * 3 + d - 1
        return remote(a1.at[c, h, (place[h] + d) % 4], c2.at[c, h, d - 1], ss2.at[c, k], rs2.at[c, k], axis_of(h)(d))

    def copy3(c, h, d):
        k = h * 3 + d - 1
        return remote(a2.at[c, h, (place[1 - h] + d) % 4], c3.at[c, h, d - 1], ss3.at[c, k], rs3.at[c, k], axis_of(1 - h)(d))

    def copy4(c, d):
        to = (z + d) % 8
        return remote(a3.at[c, to % 2, to // 2], c4.at[c, d - 1], ss4.at[c, d - 1], rs4.at[c, d - 1], device(x, y, to, core))

    def start1(c, carry):
        copy1(c).start()
        return carry

    def step1(c, carry):
        copy1(c).wait_recv()
        for h in range(2):
            def add(i, carry):
                a1[c, h, i] = (f[c, core, h, i].astype(F32) + c1[c, h, i].astype(F32)).astype(BF16)
                return carry
            lax.fori_loop(0, 4, add, 0)
            for d in (1, 2, 3):
                copy2(c, h, d).start()
        return carry

    def step2(c, carry):
        for h in range(2):
            for d in (1, 2, 3):
                copy2(c, h, d).wait_recv()
            def add(i, carry):
                v = f[c, core, h, place[h], pl.ds(i * 4, 4)].astype(F32) + c1[c, h, place[h], pl.ds(i * 4, 4)].astype(F32)
                for d in range(3):
                    v += c2[c, h, d, pl.ds(i * 4, 4)].astype(F32)
                a2[c, h, i] = v.astype(BF16)
                a2own[i] = v
                return carry
            lax.fori_loop(0, 4, add, 0)
            a3[c, h] = a2own[place[1 - h]]
            for d in (1, 2, 3):
                copy3(c, h, d).start()
        return carry

    def step3(c, carry):
        for h in range(2):
            for d in (1, 2, 3):
                copy3(c, h, d).wait_recv()
            v = a3[c, h]
            for d in range(3):
                v += c3[c, h, d].astype(F32)
            a3[c, h] = v
        for d in range(1, 8):
            copy4(c, d).start()
        return carry

    def step4(c, carry):
        for d in range(1, 8):
            copy4(c, d).wait_recv()
        v = a3[c, z % 2, z // 2]
        for d in range(7):
            v += c4[c, d]
        out[pl.ds(pl.multiple_of(c * 16, 16), 16), :] = v * (1.0 / 32768.0)
        return carry

    def drain(c, carry):
        copy1(c).wait_send()
        for h in range(2):
            for d in (1, 2, 3):
                copy2(c, h, d).wait_send()
                copy3(c, h, d).wait_send()
        for d in range(1, 8):
            copy4(c, d).wait_send()
        return carry

    for step in (start1, step1, step2, step3, step4, drain):
        lax.fori_loop(0, PIECES, step, 0)


def scatter(f):
    n = PIECES
    dma = pltpu.SemaphoreType.DMA
    return pl.pallas_call(
        scatter_kernel,
        in_specs=[pl.BlockSpec(memory_space=pltpu.VMEM)],
        out_specs=pl.BlockSpec(memory_space=pltpu.VMEM),
        out_shape=jax.ShapeDtypeStruct((NB, 128), F32),
        scratch_shapes=[
            pltpu.VMEM((n, 2, 4, 16, 16, 128), BF16),
            pltpu.VMEM((n, 2, 4, 16, 16, 128), BF16),
            pltpu.VMEM((n, 2, 3, 16, 16, 128), BF16),
            pltpu.VMEM((n, 2, 4, 4, 16, 128), BF16),
            pltpu.VMEM((4, 4, 16, 128), F32),
            pltpu.VMEM((n, 2, 3, 4, 16, 128), BF16),
            pltpu.VMEM((n, 2, 4, 16, 128), F32),
            pltpu.VMEM((n, 7, 16, 128), F32),
            dma((n,)), dma((n,)), dma((n, 6)), dma((n, 6)), dma((n, 6)), dma((n, 6)), dma((n, 7)), dma((n, 7)),
        ],
        compiler_params=pltpu.CompilerParams(
            vmem_limit_bytes=VMEM_LIMIT, collective_id=0, has_side_effects=True
        ),
        name="scatter",
    )(f.reshape(n, 2, 2, 4, 16, 16, 128))


BASES = (-1, 3, 7, 10)
COUNTS = (6, 5, 5, 6)


def sums_kernel(g, wext, gw, cols, extra, s, pa, acc, pb, tot, pc, ssa, rsa, ssb, rsb, ssc, rsc, ssg, rsg):
    x, y, z, core = coords()
    r = lax.axis_index("rep")
    p = lax.axis_index("dp")
    group, a = p // 4, p % 4
    q = a * 4 + r
    row = 15 * group + q
    ka, kb = z * 2 + core, x * 4 + y
    in_a = lambda d: (lambda k: device(x, y, k // 2, k % 2))((ka + d) % 16)
    in_b = lambda d: (lambda k: device(k // 4, k % 4, z, core))((kb + d) % 16)

    barrier = pltpu.get_barrier_semaphore()

    def hello(target):
        pl.semaphore_signal(barrier, inc=1, device_id=target, device_id_type=pl.DeviceIdType.MESH)

    for d in range(1, 16):
        hello(in_a(d))
        hello(in_b(d))
    hello({"rep": 3 - r, "dp": p})

    @pl.when(p > 0)
    def _():
        for k in range(4):
            hello({"rep": k, "dp": jnp.maximum(p - 1, 0)})

    @pl.when(p < 63)
    def _():
        for k in range(4):
            hello({"rep": k, "dp": jnp.minimum(p + 1, 63)})

    pl.semaphore_wait(barrier, 31 + 4 * jnp.where(p > 0, 1, 0) + 4 * jnp.where(p < 63, 1, 0))

    def give(fn):
        for t in range(6):
            if t < 4:
                owner, k = 4 * group + t, q - BASES[t]
                ok = (k >= 0) & (k < COUNTS[t]) & (q < 15)
                k = jnp.clip(k, 0, 5)
            elif t == 4:
                owner, k, ok = jnp.maximum(p - a - 1, 0), 5, (q == 0) & (p > 0)
            else:
                owner, k, ok = jnp.minimum(p - a + 4, 63), 0, (q == 14) & (p < 60)
            for rr in range(4):
                fn(owner, k, ok, rr, t * 4 + rr)

    def send_row(owner, k, ok, rr, n):
        @pl.when(ok & ((owner != p) | (rr != r)))
        def _():
            remote(g, gw.at[k], ssg.at[n], rsg.at[k], {"rep": rr, "dp": owner}).start()
        @pl.when(ok & (owner == p) & (rr == r))
        def _():
            gw[k] = g[...]

    give(send_row)

    sq = g[...] * g[...]
    total = jnp.sum(sq)
    lane = lax.broadcasted_iota(jnp.int32, (1, 128), 1)
    last = jnp.where(lane == row % RB, total, 0.0) * jnp.where(q < 15, 1.0, 0.0) + wext[0:1, :]
    for k in range(16):
        s[k, 0:7, :] = sq[7 * k : 7 * k + 7, :]
        s[k, 7:8, :] = last

    def copy_a(d):
        return remote(s.at[(ka + d) % 16], pa.at[d - 1], ssa.at[d - 1], rsa.at[d - 1], in_a(d))

    def copy_b(d):
        return remote(acc, pb.at[d - 1], ssb.at[d - 1], rsb.at[d - 1], in_b(d))

    def copy_c(d):
        return remote(tot, pc.at[d - 1], ssc.at[d - 1], rsc.at[d - 1], in_a(d))

    for d in range(1, 16):
        copy_a(d).start()

    def matrix_at(k):
        pp = p - z + k // 2
        rr = r - core + k % 2
        return jnp.minimum(15 * (pp // 4) + (pp % 4) * 4 + rr, 239) // RB

    v = s[ka]
    own = matrix_at(ka)
    for m in range(3):
        acc[m] = jnp.where(own == m, v, 0.0)
    for d in range(1, 16):
        copy_a(d).wait_recv()
        v = pa[d - 1]
        m_src = matrix_at((ka + 16 - d) % 16)
        for m in range(3):
            acc[m] += jnp.where(m_src == m, v, 0.0)
    for d in range(1, 16):
        copy_b(d).start()
    tot[...] = acc[...]
    for d in range(1, 16):
        copy_b(d).wait_recv()
        tot[...] += pb[d - 1]
    for d in range(1, 16):
        copy_c(d).start()

    def place(k, v):
        for m in range(3):
            cols[m, k] = v[m]

    place(ka, tot[...])
    extra[...] = tot[...]
    for d in range(1, 16):
        copy_c(d).wait_recv()
        place((ka + 16 - d) % 16, pc[d - 1])

    for k in range(6):
        if k == 0:
            ok = (p % 4 != 0) | (p > 0)
        elif k == 5:
            ok = (a == 0) | ((a == 3) & (p < 63))
        else:
            ok = a >= 0
        source_q = jnp.where(a == 0, k - 1, jnp.where(a == 1, k + 3, jnp.where(a == 2, k + 7, k + 10)))
        @pl.when(ok & ((source_q != q) | (source_q > 14)))
        def _():
            remote(g, gw.at[k], ssg.at[k], rsg.at[k], {"rep": (r + 1) % 4, "dp": p}).wait_recv()
        @pl.when(jnp.logical_not(ok))
        def _():
            gw[k] = jnp.zeros((NB, 128), F32)

    def wait_row(owner, k, ok, rr, n):
        @pl.when(ok & ((owner != p) | (rr != r)))
        def _():
            remote(g, gw.at[k], ssg.at[n], rsg.at[k], {"rep": rr, "dp": owner}).wait_send()

    give(wait_row)
    for d in range(1, 16):
        copy_a(d).wait_send()
        copy_b(d).wait_send()
        copy_c(d).wait_send()


def sums(g, wext):
    dma = pltpu.SemaphoreType.DMA
    vm = pl.BlockSpec(memory_space=pltpu.VMEM)
    return pl.pallas_call(
        sums_kernel,
        in_specs=[vm, vm],
        out_specs=[vm, vm, vm],
        out_shape=[
            jax.ShapeDtypeStruct((6, NB, 128), F32),
            jax.ShapeDtypeStruct((3, 16, 8, 128), F32),
            jax.ShapeDtypeStruct((3, 8, 128), F32),
        ],
        scratch_shapes=[
            pltpu.VMEM((16, 8, 128), F32),
            pltpu.VMEM((15, 8, 128), F32),
            pltpu.VMEM((3, 8, 128), F32),
            pltpu.VMEM((15, 3, 8, 128), F32),
            pltpu.VMEM((3, 8, 128), F32),
            pltpu.VMEM((15, 3, 8, 128), F32),
            dma((15,)), dma((15,)), dma((15,)), dma((15,)), dma((15,)), dma((15,)), dma((24,)), dma((6,)),
        ],
        compiler_params=pltpu.CompilerParams(
            vmem_limit_bytes=VMEM_LIMIT, collective_id=1, has_side_effects=True
        ),
        name="sums",
    )(g, wext)


def update_kernel(place, gw, cols, extra, params, row_state, col_state, out_p, out_d, out_r, out_c, moved, scaled):
    shift, length, first = place[0], place[1], place[2]
    for m in range(3):
        for k in range(16):
            part = pl.ds(m * NB + 7 * k, 7)
            out_c[part, :] = BETA * col_state[part, :] + (1.0 - BETA) * (cols[m, k, 0:7, :] * (1.0 / RB) + TINY)
    lane = lax.broadcasted_iota(jnp.int32, (1, 128), 1)
    sums_row = extra[:, 7, :]
    live = lax.broadcasted_iota(jnp.int32, (3, 128), 1) < RB
    rows = jnp.where(live, BETA * row_state[...] + (1.0 - BETA) * (sums_row * (1.0 / 14336.0) + TINY), 0.0)
    out_r[...] = rows
    means = jnp.sum(rows, axis=1, keepdims=True) * (1.0 / RB)
    weight = jnp.sum(sums_row, axis=0, keepdims=True)
    for k in range(6):
        row = jnp.clip(first + k, 0, 239)
        m = row // RB
        i = row % RB
        pick = lambda v: jnp.where(m == 0, v[0:1], jnp.where(m == 1, v[1:2], v[2:3]))
        value = jnp.sum(jnp.where(lane == i, pick(rows), 0.0), axis=1, keepdims=True)
        sq = jnp.sum(jnp.where(lane == 120 + m, weight, 0.0), axis=1, keepdims=True)
        scale = RHO * jnp.sqrt(sq * (1.0 / (RB * 14336.0)))
        factor = value / pick(means)
        v = gw[k] * lax.rsqrt(factor * out_c[pl.ds(pl.multiple_of(m * NB, 8), NB), :])
        moved[pl.ds(k * NB, NB), :] = v
        scaled[pl.ds(k * NB, NB), :] = scale * v
    def tile(t, carry):
        o = pl.multiple_of(t * 16, 16)
        at = pl.ds(shift + o, 16)
        keep = o + lax.broadcasted_iota(jnp.int32, (16, 128), 0) < length
        out_d[pl.ds(o, 16), :] = jnp.where(keep, moved[at, :], 0.0).astype(BF16)
        new = params[pl.ds(o, 16), :].astype(F32) - scaled[at, :]
        out_p[pl.ds(o, 16), :] = jnp.where(keep, new, 0.0).astype(BF16)
        return carry
    lax.fori_loop(0, 34, tile, 0)


def update(place, gw, cols, extra, params, row_state, col_state):
    vm = pl.BlockSpec(memory_space=pltpu.VMEM)
    return pl.pallas_call(
        update_kernel,
        in_specs=[pl.BlockSpec(memory_space=pltpu.SMEM)] + [vm] * 6,
        out_specs=[vm] * 4,
        out_shape=[
            jax.ShapeDtypeStruct((544, 128), BF16),
            jax.ShapeDtypeStruct((544, 128), BF16),
            jax.ShapeDtypeStruct((3, 128), F32),
            jax.ShapeDtypeStruct((336, 128), F32),
        ],
        scratch_shapes=[pltpu.VMEM((800, 128), F32), pltpu.VMEM((800, 128), F32)],
        compiler_params=pltpu.CompilerParams(vmem_limit_bytes=VMEM_LIMIT),
        name="update",
    )(place, gw, cols, extra, params, row_state, col_state)


def body(tokens, upstream, gate_pre, up_pre, param_shards, shard_rows, row_state, col_state):
    p = lax.axis_index("dp")
    ends = jnp.cumsum(shard_rows)
    start = ends[p] - shard_rows[p]
    length = shard_rows[p]
    capacity = param_shards.shape[0]
    offsets = jnp.arange(capacity, dtype=jnp.int32)[:, None]
    masked = jnp.where(offsets < length, param_shards, jnp.zeros_like(param_shards))
    window = lax.dynamic_slice_in_dim(
        jnp.pad(masked, ((2 * JIT, 0), (0, 0))), 2 * JIT - (start - (EV * p - JIT)), WIN, 0
    )
    wwin = lax.all_gather(window, "dp", axis=0)[FIRST:]
    squares = jnp.sum(jnp.square(masked.astype(F32)), axis=1, keepdims=True)
    flat = start + offsets
    parts = [jnp.sum(jnp.where((flat >= m * 8960) & (flat < m * 8960 + 8960), squares, 0.0)) for m in range(3)]
    lane = jnp.arange(128)[None, :]
    wext = sum(jnp.where(lane == 120 + m, parts[m] * 0.25, 0.0) for m in range(3))
    wext = jnp.broadcast_to(wext, (8, 128))
    f = grads(tokens, upstream, gate_pre, up_pre, wwin)
    g = scatter(f)
    gw, cols, extra = sums(g, wext)
    a = p % 4
    first = 15 * (p // 4) + jnp.where(a == 0, -1, jnp.where(a == 1, 3, jnp.where(a == 2, 7, 10)))
    place = jnp.stack([start - NB * first, length, first]).astype(jnp.int32)
    row_in = jnp.pad(row_state.reshape(3, RB), ((0, 0), (0, 128 - RB)))
    new_params, direction, rows, new_cols = update(
        place, gw, cols, extra, param_shards, row_in, col_state.reshape(336, 128)
    )
    return (new_params, direction, rows[:, :RB].reshape(-1), new_cols.reshape(-1))


def solution(mesh):
    in_specs = (
        P(("rep", "dp"), None),
        P(("rep", "dp"), None),
        P(("rep", "dp"), None),
        P(("rep", "dp"), None),
        P("dp", None),
        P(),
        P(),
        P(),
    )
    out_specs = (P("dp", None), P("dp", None), P(), P())
    return jax.shard_map(body, mesh=mesh, in_specs=in_specs, out_specs=out_specs, check_vma=False)
```

```python
import functools

import jax
import jax.numpy as jnp
from jax import lax
from jax.experimental import pallas as pl
from jax.experimental.pallas import tpu as pltpu
from jax.sharding import PartitionSpec as P

BETA = 0.8
RHO = 0.2
TINY = 1e-30
RB = 80
NB = 112
EV = 420
JIT = 52
WIN = 528
FIRST = 42
NWIN = 22
PIECES = 7
SLOTS = 256
WPAD = 336
WROWS = 9360
F32 = jnp.float32
BF16 = jnp.bfloat16
VMEM_LIMIT = 56 * 1024 * 1024


def slot_row(pos):
    zz = pos % 4
    second = pos // 4 % 4
    first = pos // 16 % 4
    h = pos // 64 % 2
    core = pos // 128
    z = 2 * zz + h
    x, y = (first, second) if h == 0 else (second, first)
    p = (x * 2 + y // 2) * 8 + z
    r = (y % 2) * 2 + core
    q = (p % 4) * 4 + r
    return None if q == 15 else 15 * (p // 4) + q


def coords():
    r = lax.axis_index("rep")
    p = lax.axis_index("dp")
    x = p // 16
    y = (p // 8 % 2) * 2 + r // 2
    return x, y, p % 8, r % 2


def device(x, y, z, core):
    return {"rep": (y % 2) * 2 + core, "dp": (x * 2 + y // 2) * 8 + z}


def span(lengths):
    p = lax.axis_index("dp")
    start = lax.fori_loop(0, p, lambda k, total: total + lengths[k], jnp.int32(0))
    return start, lengths[p]


def prep_kernel(lengths, params, quarter, wext, shifted):
    p, r = lax.axis_index("dp"), lax.axis_index("rep")
    start, length = span(lengths)
    row = lax.broadcasted_iota(jnp.int32, (544, 128), 0)
    v = jnp.where(row < length, params[...].astype(F32), 0.0)
    shifted[0 : 2 * JIT, :] = jnp.zeros((2 * JIT, 128), F32)
    shifted[2 * JIT : 2 * JIT + 544, :] = v
    shifted[2 * JIT + 544 :, :] = jnp.zeros((72, 128), F32)
    at = 2 * JIT - (start - (EV * p - JIT)) + 144 * r
    quarter[...] = shifted[pl.ds(at, 144), :].astype(BF16)
    v = v * v
    flat = row + start
    lane = lax.broadcasted_iota(jnp.int32, (8, 128), 1)
    total = jnp.zeros((8, 128), F32)
    for m in range(3):
        inside = (flat >= m * 8960) & (flat < m * 8960 + 8960)
        total += jnp.where(lane == 120 + m, 0.25 * jnp.sum(jnp.where(inside, v, 0.0)), 0.0)
    wext[...] = total


def prep(shard_rows, params):
    vm = pl.BlockSpec(memory_space=pltpu.VMEM)
    return pl.pallas_call(
        prep_kernel,
        in_specs=[pl.BlockSpec(memory_space=pltpu.SMEM), vm],
        out_specs=[vm, vm],
        out_shape=[jax.ShapeDtypeStruct((144, 128), BF16), jax.ShapeDtypeStruct((8, 128), F32)],
        scratch_shapes=[pltpu.VMEM((720, 128), F32)],
        compiler_params=pltpu.CompilerParams(vmem_limit_bytes=VMEM_LIMIT),
        name="prep",
    )(shard_rows, params)


def gather_kernel(quarter, w, s1, r1, sp, rp, sm, rm, sy, ry, sc, rc):
    x, y, z, core = coords()
    r, p = lax.axis_index("rep"), lax.axis_index("dp")
    plane = p // 8
    spread = lambda d: {"rep": r, "dp": (plane + d) % 8 * 8 + z}
    up, down = device(x, y, (z + 1) % 8, core), device(x, y, (z + 7) % 8, core)
    north, south = device(x, (y + 1) % 4, z, core), device(x, (y + 3) % 4, z, core)
    other = device(x, y, z, 1 - core)
    greet([spread(d) for d in range(1, 8)] + [up, down, north, south, other])
    mate = (1 - r // 2) * 2 + core

    def copy1(d):
        u = jnp.maximum(plane - 5, 0)
        return remote(quarter, w.at[z, r, u], s1.at[d - 1], r1.at[u], spread(d))

    def copy_up(s):
        o = (z + 9 - s) % 8
        return remote(w.at[o, r], w.at[o, r], sp.at[s - 1], rp.at[s - 1], up)

    def copy_down(s):
        o = (z + s - 1) % 8
        return remote(w.at[o, r], w.at[o, r], sm.at[s - 1], rm.at[s - 1], down)

    def copy_y(k):
        o = (z + 8 - k) % 8
        to = south if k in (0, 5, 6, 7) else north
        return remote(w.at[o, r], w.at[o, r], sy.at[k], ry.at[k], to)

    def copy_core(k, quarter_of, n):
        o = (z + 8 - k) % 8
        return remote(w.at[o, quarter_of], w.at[o, quarter_of], sc.at[n], rc.at[n], other)

    holds = p >= 40

    @pl.when(holds)
    def _():
        for d in range(1, 8):
            copy1(d).start()
        w[z, r, jnp.maximum(plane - 5, 0)] = quarter[...]

    for u in range(3):
        @pl.when(plane != 5 + u)
        def _():
            remote(quarter, w.at[z, r, u], s1.at[0], r1.at[u], spread(1)).wait_recv()

    copy_up(1).start()
    copy_down(1).start()
    copy_y(0).start()
    copy_core(0, r, 0).start()
    for s in range(1, 5):
        copy_up(s).wait_recv()
        if s < 4:
            copy_up(s + 1).start()
        copy_y(s).start()
        copy_core(s, r, s).start()
        if s < 4:
            copy_down(s).wait_recv()
            if s < 3:
                copy_down(s + 1).start()
            copy_y(8 - s).start()
            copy_core(8 - s, r, 8 - s).start()
    for k in (0, 1, 7, 2, 6, 3, 5, 4):
        copy_y(k).wait_recv()
        copy_core(k, mate, 8 + k).start()
    for k in range(8):
        copy_core(k, r, k).wait_recv()
        copy_core(k, mate, 8 + k).wait_recv()

    @pl.when(holds)
    def _():
        for d in range(1, 8):
            copy1(d).wait_send()

    for s in range(1, 5):
        copy_up(s).wait_send()
        if s < 4:
            copy_down(s).wait_send()
    for k in range(8):
        copy_y(k).wait_send()
        copy_core(k, r, k).wait_send()
        copy_core(k, mate, 8 + k).wait_send()


def gather(quarter):
    dma = pltpu.SemaphoreType.DMA
    vm = pl.BlockSpec(memory_space=pltpu.VMEM)
    return pl.pallas_call(
        gather_kernel,
        in_specs=[vm],
        out_specs=vm,
        out_shape=jax.ShapeDtypeStruct((8, 4, 3, 144, 128), BF16),
        scratch_shapes=[dma((n,)) for n in (7, 3, 4, 4, 3, 3, 8, 8, 16, 16)],
        compiler_params=pltpu.CompilerParams(
            vmem_limit_bytes=VMEM_LIMIT, collective_id=2, has_side_effects=True
        ),
        name="gather",
    )(quarter)


def grads_kernel(tok_t, up_t, up, wwin, gate, upp, out, wflat, rows):
    c = pl.program_id(0)

    @pl.when(c == 0)
    def _():
        for n in range(NWIN):
            off = EV * (FIRST + n) - JIT - 17920 + WPAD
            u, zz = (FIRST + n - 40) // 8, (FIRST + n) % 8
            for r in range(4):
                for t in range(9 if r < 3 else 6):
                    v = wwin[zz, r, u, t * 16 : t * 16 + 16, :].astype(F32)
                    first = r * 144 + t * 16
                    for half in range(2):
                        if n and first + half * 8 < 2 * JIT:
                            wflat[pl.ds(off + first + half * 8, 8), :] += v[half * 8 : half * 8 + 8]
                        else:
                            wflat[pl.ds(off + first + half * 8, 8), :] = v[half * 8 : half * 8 + 8]

    def block(jj, carry):
        cols = pl.ds(pl.multiple_of(jj * 256, 256), 256)
        g = gate[:, cols].astype(F32)
        u = upp[:, cols].astype(F32)
        s = 0.5 * jnp.tanh(0.5 * g) + 0.5
        act = g * s
        hid = (act * u).astype(BF16)
        gd = jnp.dot(up_t[...], hid, preferred_element_type=F32)
        j = c * 16 + jj * 2
        w = jnp.concatenate(
            [wflat[pl.ds(WPAD + j + b, RB, stride=NB), :] for b in range(2)], axis=1
        ).astype(BF16)
        dh = jnp.dot(up[...], w, preferred_element_type=F32)
        dg = (dh * u * s * (1.0 + g * (1.0 - s))).astype(BF16)
        du = (dh * act).astype(BF16)
        gg = jnp.dot(tok_t[...], dg, preferred_element_type=F32)
        gu = jnp.dot(tok_t[...], du, preferred_element_type=F32)
        for m, v in enumerate((gg, gu, gd)):
            for b in range(2):
                rows[pl.ds(m * RB * 16 + jj * 2 + b, RB, stride=16), :] = v[:, b * 128 : b * 128 + 128]
        return carry

    lax.fori_loop(0, 8, block, 0)
    for pos in range(SLOTS):
        row = slot_row(pos)
        if row is None:
            out[0, pos] = jnp.zeros((16, 128), BF16)
        else:
            out[0, pos] = rows[row * 16 : row * 16 + 16, :].astype(BF16)


def grads(tokens, upstream, gate_pre, up_pre, wwin):
    whole = lambda shape: pl.BlockSpec(shape, lambda c: (0,) * len(shape))
    return pl.pallas_call(
        grads_kernel,
        grid=(PIECES,),
        in_specs=[
            whole((RB, 128)),
            whole((RB, 128)),
            whole((128, RB)),
            whole((8, 4, 3, 144, 128)),
            pl.BlockSpec((128, 2048), lambda c: (0, c)),
            pl.BlockSpec((128, 2048), lambda c: (0, c)),
        ],
        out_specs=pl.BlockSpec((1, SLOTS, 16, 128), lambda c: (c, 0, 0, 0)),
        out_shape=jax.ShapeDtypeStruct((PIECES, SLOTS, 16, 128), BF16),
        scratch_shapes=[pltpu.VMEM((WROWS, 128), F32), pltpu.VMEM((240 * 16, 128), F32)],
        compiler_params=pltpu.CompilerParams(vmem_limit_bytes=VMEM_LIMIT),
        name="grads",
    )(tokens.T, upstream.T, upstream, wwin, gate_pre, up_pre)


def greet(targets):
    barrier = pltpu.get_barrier_semaphore()
    for target in targets:
        pl.semaphore_signal(barrier, inc=1, device_id=target, device_id_type=pl.DeviceIdType.MESH)
    pl.semaphore_wait(barrier, len(targets))


def remote(src, dst, send, recv, target):
    return pltpu.make_async_remote_copy(
        src_ref=src, dst_ref=dst, send_sem=send, recv_sem=recv,
        device_id=target, device_id_type=pl.DeviceIdType.MESH,
    )


def scatter_kernel(f, out, c1, a1, c2, a2, a2own, c3, a3, c4, ss1, rs1, ss2, rs2, ss3, rs3, ss4, rs4):
    x, y, z, core = coords()
    axis_of = lambda h: (lambda d: device((x + d) % 4, y, z, core)) if h == 0 else (
        lambda d: device(x, (y + d) % 4, z, core))
    place = (x, y)
    greet(
        [device(x, y, z, 1 - core)]
        + [axis_of(h)(d) for h in range(2) for d in (1, 2, 3)]
        + [device(x, y, (z + d) % 8, core) for d in range(1, 8)]
    )

    def copy1(c):
        return remote(f.at[c, 1 - core], c1.at[c], ss1.at[c], rs1.at[c], device(x, y, z, 1 - core))

    def copy2(c, h, d):
        k = h * 3 + d - 1
        return remote(a1.at[c, h, (place[h] + d) % 4], c2.at[c, h, d - 1], ss2.at[c, k], rs2.at[c, k], axis_of(h)(d))

    def copy3(c, h, d):
        k = h * 3 + d - 1
        return remote(a2.at[c, h, (place[1 - h] + d) % 4], c3.at[c, h, d - 1], ss3.at[c, k], rs3.at[c, k], axis_of(1 - h)(d))

    def copy4(c, d):
        to = (z + d) % 8
        return remote(a3.at[c, to % 2, to // 2], c4.at[c, d - 1], ss4.at[c, d - 1], rs4.at[c, d - 1], device(x, y, to, core))

    def start1(c, carry):
        copy1(c).start()
        return carry

    def step1(c, carry):
        copy1(c).wait_recv()
        for h in range(2):
            def add(i, carry):
                a1[c, h, i] = (f[c, core, h, i].astype(F32) + c1[c, h, i].astype(F32)).astype(BF16)
                return carry
            lax.fori_loop(0, 4, add, 0)
            for d in (1, 2, 3):
                copy2(c, h, d).start()
        return carry

    def step2(c, carry):
        for h in range(2):
            for d in (1, 2, 3):
                copy2(c, h, d).wait_recv()
            def add(i, carry):
                v = f[c, core, h, place[h], pl.ds(i * 4, 4)].astype(F32) + c1[c, h, place[h], pl.ds(i * 4, 4)].astype(F32)
                for d in range(3):
                    v += c2[c, h, d, pl.ds(i * 4, 4)].astype(F32)
                a2[c, h, i] = v.astype(BF16)
                a2own[i] = v
                return carry
            lax.fori_loop(0, 4, add, 0)
            a3[c, h] = a2own[place[1 - h]]
            for d in (1, 2, 3):
                copy3(c, h, d).start()
        return carry

    def step3(c, carry):
        for h in range(2):
            for d in (1, 2, 3):
                copy3(c, h, d).wait_recv()
            v = a3[c, h]
            for d in range(3):
                v += c3[c, h, d].astype(F32)
            a3[c, h] = v
        for d in range(1, 8):
            copy4(c, d).start()
        return carry

    def step4(c, carry):
        for d in range(1, 8):
            copy4(c, d).wait_recv()
        v = a3[c, z % 2, z // 2]
        for d in range(7):
            v += c4[c, d]
        out[pl.ds(pl.multiple_of(c * 16, 16), 16), :] = v * (1.0 / 32768.0)
        return carry

    def drain(c, carry):
        copy1(c).wait_send()
        for h in range(2):
            for d in (1, 2, 3):
                copy2(c, h, d).wait_send()
                copy3(c, h, d).wait_send()
        for d in range(1, 8):
            copy4(c, d).wait_send()
        return carry

    for step in (start1, step1, step2, step3, step4, drain):
        lax.fori_loop(0, PIECES, step, 0)


def scatter(f):
    n = PIECES
    dma = pltpu.SemaphoreType.DMA
    return pl.pallas_call(
        scatter_kernel,
        in_specs=[pl.BlockSpec(memory_space=pltpu.VMEM)],
        out_specs=pl.BlockSpec(memory_space=pltpu.VMEM),
        out_shape=jax.ShapeDtypeStruct((NB, 128), F32),
        scratch_shapes=[
            pltpu.VMEM((n, 2, 4, 16, 16, 128), BF16),
            pltpu.VMEM((n, 2, 4, 16, 16, 128), BF16),
            pltpu.VMEM((n, 2, 3, 16, 16, 128), BF16),
            pltpu.VMEM((n, 2, 4, 4, 16, 128), BF16),
            pltpu.VMEM((4, 4, 16, 128), F32),
            pltpu.VMEM((n, 2, 3, 4, 16, 128), BF16),
            pltpu.VMEM((n, 2, 4, 16, 128), F32),
            pltpu.VMEM((n, 7, 16, 128), F32),
            dma((n,)), dma((n,)), dma((n, 6)), dma((n, 6)), dma((n, 6)), dma((n, 6)), dma((n, 7)), dma((n, 7)),
        ],
        compiler_params=pltpu.CompilerParams(
            vmem_limit_bytes=VMEM_LIMIT, collective_id=0, has_side_effects=True
        ),
        name="scatter",
    )(f.reshape(n, 2, 2, 4, 16, 16, 128))


BASES = (-1, 3, 7, 10)
COUNTS = (6, 5, 5, 6)


def sums_kernel(g, wext, gw, cols, extra, s, pa, acc, pb, tot, pc, ssa, rsa, ssb, rsb, ssc, rsc, ssg, rsg):
    x, y, z, core = coords()
    r = lax.axis_index("rep")
    p = lax.axis_index("dp")
    group, a = p // 4, p % 4
    q = a * 4 + r
    row = 15 * group + q
    ka, kb = z * 2 + core, x * 4 + y
    in_a = lambda d: (lambda k: device(x, y, k // 2, k % 2))((ka + d) % 16)
    in_b = lambda d: (lambda k: device(k // 4, k % 4, z, core))((kb + d) % 16)

    barrier = pltpu.get_barrier_semaphore()

    def hello(target):
        pl.semaphore_signal(barrier, inc=1, device_id=target, device_id_type=pl.DeviceIdType.MESH)

    for d in range(1, 16):
        hello(in_a(d))
        hello(in_b(d))
    hello({"rep": 3 - r, "dp": p})

    @pl.when(p > 0)
    def _():
        for k in range(4):
            hello({"rep": k, "dp": jnp.maximum(p - 1, 0)})

    @pl.when(p < 63)
    def _():
        for k in range(4):
            hello({"rep": k, "dp": jnp.minimum(p + 1, 63)})

    pl.semaphore_wait(barrier, 31 + 4 * jnp.where(p > 0, 1, 0) + 4 * jnp.where(p < 63, 1, 0))

    def give(fn):
        for t in range(6):
            if t < 4:
                owner, k = 4 * group + t, q - BASES[t]
                ok = (k >= 0) & (k < COUNTS[t]) & (q < 15)
                k = jnp.clip(k, 0, 5)
            elif t == 4:
                owner, k, ok = jnp.maximum(p - a - 1, 0), 5, (q == 0) & (p > 0)
            else:
                owner, k, ok = jnp.minimum(p - a + 4, 63), 0, (q == 14) & (p < 60)
            for rr in range(4):
                fn(owner, k, ok, rr, t * 4 + rr)

    def send_row(owner, k, ok, rr, n):
        @pl.when(ok & ((owner != p) | (rr != r)))
        def _():
            remote(g, gw.at[k], ssg.at[n], rsg.at[k], {"rep": rr, "dp": owner}).start()
        @pl.when(ok & (owner == p) & (rr == r))
        def _():
            gw[k] = g[...]

    give(send_row)

    sq = g[...] * g[...]
    total = jnp.sum(sq)
    lane = lax.broadcasted_iota(jnp.int32, (1, 128), 1)
    last = jnp.where(lane == row % RB, total, 0.0) * jnp.where(q < 15, 1.0, 0.0) + wext[0:1, :]
    for k in range(16):
        s[k, 0:7, :] = sq[7 * k : 7 * k + 7, :]
        s[k, 7:8, :] = last

    def copy_a(d):
        return remote(s.at[(ka + d) % 16], pa.at[d - 1], ssa.at[d - 1], rsa.at[d - 1], in_a(d))

    def copy_b(d):
        return remote(acc, pb.at[d - 1], ssb.at[d - 1], rsb.at[d - 1], in_b(d))

    def copy_c(d):
        return remote(tot, pc.at[d - 1], ssc.at[d - 1], rsc.at[d - 1], in_a(d))

    for d in range(1, 16):
        copy_a(d).start()

    def matrix_at(k):
        pp = p - z + k // 2
        rr = r - core + k % 2
        return jnp.minimum(15 * (pp // 4) + (pp % 4) * 4 + rr, 239) // RB

    v = s[ka]
    own = matrix_at(ka)
    for m in range(3):
        acc[m] = jnp.where(own == m, v, 0.0)
    for d in range(1, 16):
        copy_a(d).wait_recv()
        v = pa[d - 1]
        m_src = matrix_at((ka + 16 - d) % 16)
        for m in range(3):
            acc[m] += jnp.where(m_src == m, v, 0.0)
    for d in range(1, 16):
        copy_b(d).start()
    tot[...] = acc[...]
    for d in range(1, 16):
        copy_b(d).wait_recv()
        tot[...] += pb[d - 1]
    for d in range(1, 16):
        copy_c(d).start()

    def place(k, v):
        for m in range(3):
            cols[m, k] = v[m]

    place(ka, tot[...])
    extra[...] = tot[...]
    for d in range(1, 16):
        copy_c(d).wait_recv()
        place((ka + 16 - d) % 16, pc[d - 1])

    for k in range(6):
        if k == 0:
            ok = (p % 4 != 0) | (p > 0)
        elif k == 5:
            ok = (a == 0) | ((a == 3) & (p < 63))
        else:
            ok = a >= 0
        source_q = jnp.where(a == 0, k - 1, jnp.where(a == 1, k + 3, jnp.where(a == 2, k + 7, k + 10)))
        @pl.when(ok & ((source_q != q) | (source_q > 14)))
        def _():
            remote(g, gw.at[k], ssg.at[k], rsg.at[k], {"rep": (r + 1) % 4, "dp": p}).wait_recv()
        @pl.when(jnp.logical_not(ok))
        def _():
            gw[k] = jnp.zeros((NB, 128), F32)

    def wait_row(owner, k, ok, rr, n):
        @pl.when(ok & ((owner != p) | (rr != r)))
        def _():
            remote(g, gw.at[k], ssg.at[n], rsg.at[k], {"rep": rr, "dp": owner}).wait_send()

    give(wait_row)
    for d in range(1, 16):
        copy_a(d).wait_send()
        copy_b(d).wait_send()
        copy_c(d).wait_send()


def sums(g, wext):
    dma = pltpu.SemaphoreType.DMA
    vm = pl.BlockSpec(memory_space=pltpu.VMEM)
    return pl.pallas_call(
        sums_kernel,
        in_specs=[vm, vm],
        out_specs=[vm, vm, vm],
        out_shape=[
            jax.ShapeDtypeStruct((6, NB, 128), F32),
            jax.ShapeDtypeStruct((3, 16, 8, 128), F32),
            jax.ShapeDtypeStruct((3, 8, 128), F32),
        ],
        scratch_shapes=[
            pltpu.VMEM((16, 8, 128), F32),
            pltpu.VMEM((15, 8, 128), F32),
            pltpu.VMEM((3, 8, 128), F32),
            pltpu.VMEM((15, 3, 8, 128), F32),
            pltpu.VMEM((3, 8, 128), F32),
            pltpu.VMEM((15, 3, 8, 128), F32),
            dma((15,)), dma((15,)), dma((15,)), dma((15,)), dma((15,)), dma((15,)), dma((24,)), dma((6,)),
        ],
        compiler_params=pltpu.CompilerParams(
            vmem_limit_bytes=VMEM_LIMIT, collective_id=1, has_side_effects=True
        ),
        name="sums",
    )(g, wext)


def update_kernel(lengths, gw, cols, extra, params, row_state, col_state, out_p, out_d, out_r, out_c, moved, scaled):
    p = lax.axis_index("dp")
    start, length = span(lengths)
    a = p % 4
    first = 15 * (p // 4) + jnp.where(a == 0, -1, jnp.where(a == 1, 3, jnp.where(a == 2, 7, 10)))
    shift = start - NB * first
    for m in range(3):
        for k in range(16):
            part = pl.ds(m * NB + 7 * k, 7)
            out_c[part, :] = BETA * col_state[part, :] + (1.0 - BETA) * (cols[m, k, 0:7, :] * (1.0 / RB) + TINY)
    lane = lax.broadcasted_iota(jnp.int32, (1, 128), 1)
    sums_row = extra[:, 7, :]
    live = lax.broadcasted_iota(jnp.int32, (3, 128), 1) < RB
    rows = jnp.where(live, BETA * row_state[...] + (1.0 - BETA) * (sums_row * (1.0 / 14336.0) + TINY), 0.0)
    out_r[...] = rows
    means = jnp.sum(rows, axis=1, keepdims=True) * (1.0 / RB)
    weight = jnp.sum(sums_row, axis=0, keepdims=True)
    for k in range(6):
        row = jnp.clip(first + k, 0, 239)
        m = row // RB
        i = row % RB
        pick = lambda v: jnp.where(m == 0, v[0:1], jnp.where(m == 1, v[1:2], v[2:3]))
        value = jnp.sum(jnp.where(lane == i, pick(rows), 0.0), axis=1, keepdims=True)
        sq = jnp.sum(jnp.where(lane == 120 + m, weight, 0.0), axis=1, keepdims=True)
        scale = RHO * jnp.sqrt(sq * (1.0 / (RB * 14336.0)))
        factor = value / pick(means)
        v = gw[k] * lax.rsqrt(factor * out_c[pl.ds(pl.multiple_of(m * NB, 8), NB), :])
        moved[pl.ds(k * NB, NB), :] = v
        scaled[pl.ds(k * NB, NB), :] = scale * v
    def tile(t, carry):
        o = pl.multiple_of(t * 16, 16)
        at = pl.ds(shift + o, 16)
        keep = o + lax.broadcasted_iota(jnp.int32, (16, 128), 0) < length
        out_d[pl.ds(o, 16), :] = jnp.where(keep, moved[at, :], 0.0).astype(BF16)
        new = params[pl.ds(o, 16), :].astype(F32) - scaled[at, :]
        out_p[pl.ds(o, 16), :] = jnp.where(keep, new, 0.0).astype(BF16)
        return carry
    lax.fori_loop(0, 34, tile, 0)


def update(lengths, gw, cols, extra, params, row_state, col_state):
    vm = pl.BlockSpec(memory_space=pltpu.VMEM)
    return pl.pallas_call(
        update_kernel,
        in_specs=[pl.BlockSpec(memory_space=pltpu.SMEM)] + [vm] * 6,
        out_specs=[vm] * 4,
        out_shape=[
            jax.ShapeDtypeStruct((544, 128), BF16),
            jax.ShapeDtypeStruct((544, 128), BF16),
            jax.ShapeDtypeStruct((3, 128), F32),
            jax.ShapeDtypeStruct((336, 128), F32),
        ],
        scratch_shapes=[pltpu.VMEM((800, 128), F32), pltpu.VMEM((800, 128), F32)],
        compiler_params=pltpu.CompilerParams(vmem_limit_bytes=VMEM_LIMIT),
        name="update",
    )(lengths, gw, cols, extra, params, row_state, col_state)


def body(tokens, upstream, gate_pre, up_pre, param_shards, shard_rows, row_state, col_state):
    quarter, wext = prep(shard_rows, param_shards)
    wwin = gather(quarter)
    f = grads(tokens, upstream, gate_pre, up_pre, wwin)
    g = scatter(f)
    gw, cols, extra = sums(g, wext)
    row_in = jnp.pad(row_state.reshape(3, RB), ((0, 0), (0, 128 - RB)))
    new_params, direction, rows, new_cols = update(
        shard_rows, gw, cols, extra, param_shards, row_in, col_state.reshape(336, 128)
    )
    return (new_params, direction, rows[:, :RB].reshape(-1), new_cols.reshape(-1))


def solution(mesh):
    in_specs = (
        P(("rep", "dp"), None),
        P(("rep", "dp"), None),
        P(("rep", "dp"), None),
        P(("rep", "dp"), None),
        P("dp", None),
        P(),
        P(),
        P(),
    )
    out_specs = (P("dp", None), P("dp", None), P(), P())
    return jax.shard_map(body, mesh=mesh, in_specs=in_specs, out_specs=out_specs, check_vma=False)
```

```python
import functools

import jax
import jax.numpy as jnp
from jax import lax
from jax.experimental import pallas as pl
from jax.experimental.pallas import tpu as pltpu
from jax.sharding import PartitionSpec as P

BETA = 0.8
RHO = 0.2
TINY = 1e-30
RB = 80
NB = 112
EV = 420
JIT = 52
PIECES = 7
WPAD = 1176
WROWS = 10200
BASES = (-1, 3, 7, 10)
COUNTS = (6, 5, 5, 6)
F32 = jnp.float32
BF16 = jnp.bfloat16
VMEM_LIMIT = 60 * 1024 * 1024


def coords():
    r = lax.axis_index("rep")
    p = lax.axis_index("dp")
    x = p // 16
    y = (p // 8 % 2) * 2 + r // 2
    return x, y, p % 8, r % 2


def device(x, y, z, core):
    return {"rep": (y % 2) * 2 + core, "dp": (x * 2 + y // 2) * 8 + z}


def greet(targets):
    barrier = pltpu.get_barrier_semaphore()
    for target in targets:
        pl.semaphore_signal(barrier, inc=1, device_id=target, device_id_type=pl.DeviceIdType.MESH)
    pl.semaphore_wait(barrier, len(targets))


def remote(src, dst, send, recv, target):
    return pltpu.make_async_remote_copy(
        src_ref=src, dst_ref=dst, send_sem=send, recv_sem=recv,
        device_id=target, device_id_type=pl.DeviceIdType.MESH,
    )


def span(lengths):
    p = lax.axis_index("dp")
    start = lax.fori_loop(0, p, lambda k, total: total + lengths[k], jnp.int32(0))
    return start, lengths[p]


def prep_kernel(lengths, params, quarter, wext, shifted):
    p, r = lax.axis_index("dp"), lax.axis_index("rep")
    start, length = span(lengths)
    row = lax.broadcasted_iota(jnp.int32, (544, 128), 0)
    v = jnp.where(row < length, params[...].astype(F32), 0.0)
    shifted[0 : 2 * JIT, :] = jnp.zeros((2 * JIT, 128), F32)
    shifted[2 * JIT : 2 * JIT + 544, :] = v
    shifted[2 * JIT + 544 :, :] = jnp.zeros((72, 128), F32)
    at = 2 * JIT - (start - (EV * p - JIT)) + 144 * r
    quarter[...] = shifted[pl.ds(at, 144), :].astype(BF16)
    v = v * v
    flat = row + start
    lane = lax.broadcasted_iota(jnp.int32, (8, 128), 1)
    total = jnp.zeros((8, 128), F32)
    for m in range(3):
        inside = (flat >= m * 8960) & (flat < m * 8960 + 8960)
        total += jnp.where(lane == 120 + m, 0.25 * jnp.sum(jnp.where(inside, v, 0.0)), 0.0)
    wext[...] = total


def prep(shard_rows, params):
    vm = pl.BlockSpec(memory_space=pltpu.VMEM)
    return pl.pallas_call(
        prep_kernel,
        in_specs=[pl.BlockSpec(memory_space=pltpu.SMEM), vm],
        out_specs=[vm, vm],
        out_shape=[jax.ShapeDtypeStruct((144, 128), BF16), jax.ShapeDtypeStruct((8, 128), F32)],
        scratch_shapes=[pltpu.VMEM((720, 128), F32)],
        compiler_params=pltpu.CompilerParams(vmem_limit_bytes=VMEM_LIMIT),
        name="prep",
    )(shard_rows, params)


def matrix_of(n):
    return jnp.where(n < 4, 2, jnp.where(n < 9, 0, jnp.where(n < 14, 1, 2)))


def index_of(n):
    return jnp.where(n < 4, n, jnp.where(n < 9, n - 4, jnp.where(n < 14, n - 9, 4)))


def member(z, core):
    return z % 4 * 4 + z // 4 * 2 + core


def main_kernel(
    tok_t, up_t, gate_hbm, upp_hbm, quarter, wext, gw, cols, extra,
    gate, upp, act, fac, w, wflat, rows, fa, fb, c1a, c1b, a1a, a1b, c2a, c2b, a2a, a2b, own2a, own2b,
    c3a, c3b, a3, c4, up, g, sq, pa, acc, pb, tot, pc,
    sg, su, w1, v1, wp, vp, wm, vm, wy, vy, wc, vc,
    s1, r1, s2, r2, s3, r3, s4, r4, ssa, rsa, ssb, rsb, ssc, rsc, ssd, rsd, ssg, rsg,
):
    x, y, z, core = coords()
    r, p = lax.axis_index("rep"), lax.axis_index("dp")
    plane = p // 8
    other = device(x, y, z, 1 - core)
    along_x = lambda d: device((x + d) % 4, y, z, core)
    along_y = lambda d: device(x, (y + d) % 4, z, core)
    along_z = lambda d: device(x, y, (z + d) % 8, core)

    def load(c):
        part = pl.ds(pl.multiple_of(c * 2048, 2048), 2048)
        return (
            pltpu.make_async_copy(gate_hbm.at[:, part], gate.at[c], sg.at[c]),
            pltpu.make_async_copy(upp_hbm.at[:, part], upp.at[c], su.at[c]),
        )

    def begin(c, carry):
        for copy in load(c):
            copy.start()
        return carry

    lax.fori_loop(0, PIECES, begin, 0)
    greet(
        [other]
        + [along_x(d) for d in (1, 2, 3)]
        + [along_y(d) for d in (1, 2, 3)]
        + [along_z(d) for d in range(1, 8)]
        + [device((x + d) % 4, (y + 2) % 4, z, core) for d in (1, 2, 3)]
    )

    spread = lambda d: {"rep": r, "dp": (plane + d) % 8 * 8 + z}
    mate = (1 - r // 2) * 2 + core

    def copy_spread(d):
        return remote(quarter, w.at[z, r, jnp.maximum(plane - 5, 0)], w1.at[d - 1], v1.at[jnp.maximum(plane - 5, 0)], spread(d))

    def copy_up(s, u):
        block = w.at[(z + 9 - s) % 8, r, u]
        n = (s - 1) * 3 + u
        return remote(block, block, wp.at[n], vp.at[n], along_z(1))

    def copy_down(s, u):
        block = w.at[(z + s - 1) % 8, r, u]
        n = (s - 1) * 3 + u
        return remote(block, block, wm.at[n], vm.at[n], along_z(7))

    def copy_y(k, u):
        block = w.at[(z + 8 - k) % 8, r, u]
        to = jnp.where((k == 0) | (k > 4), 3, 1)
        return remote(block, block, wy.at[k * 3 + u], vy.at[k * 3 + u], along_y(to))

    def copy_core(k, q, u):
        block = w.at[(z + 8 - k) % 8, q, u]
        n = (jnp.where(q == r, 0, 8) + k) * 3 + u
        return remote(block, block, wc.at[n], vc.at[n], other)

    @pl.when(p >= 40)
    def _():
        for d in range(1, 8):
            copy_spread(d).start()
        w[z, r, jnp.maximum(plane - 5, 0)] = quarter[...]

    def gather_first():
        for u in range(3):
            @pl.when(plane != 5 + u)
            def _():
                remote(quarter, w.at[z, r, u], w1.at[0], v1.at[u], spread(1)).wait_recv()
            copy_up(1, u).start()
            copy_down(1, u).start()
            copy_y(0, u).start()
            copy_core(0, r, u).start()

    def gather_ring(s):
        for u in range(3):
            copy_up(s, u).wait_recv()
            if s < 4:
                copy_up(s + 1, u).start()
            copy_y(s, u).start()
            copy_core(s, r, u).start()
            if s < 4:
                copy_down(s, u).wait_recv()
                if s < 3:
                    copy_down(s + 1, u).start()
                copy_y(8 - s, u).start()
                copy_core(8 - s, r, u).start()

    f, c1, a1, c2 = (fa, fb), (c1a, c1b), (a1a, a1b), (c2a, c2b)
    a2, own2, c3 = (a2a, a2b), (own2a, own2b), (c3a, c3b)
    first, second = (x, y), (y, x)
    axis_of = (along_x, along_y)

    def copy1(t, c):
        k = t * PIECES + c
        return remote(f[t].at[c, 1 - core], c1[t].at[c], s1.at[k], r1.at[k], other)

    def copy2(t, c, h, d):
        k, n = t * PIECES + c, h * 3 + d - 1
        return remote(a1[t].at[c, h, (first[h] + d) % 4], c2[t].at[c, h, d - 1], s2.at[k, n], r2.at[k, n], axis_of[h](d))

    def copy3(t, c, h, d):
        k, n = t * PIECES + c, h * 3 + d - 1
        return remote(a2[t].at[c, h, (second[h] + d) % 4], c3[t].at[c, h, d - 1], s3.at[k, n], r3.at[k, n], axis_of[1 - h](d))

    def copy4(c, d):
        to = (z + d) % 8
        return remote(a3.at[c, to // 4, to % 4], c4.at[c, d - 1], s4.at[c, d - 1], r4.at[c, d - 1], along_z(d))

    def step1(t, c):
        copy1(t, c).wait_recv()
        for h in range(2):
            def add(i, carry):
                a1[t][c, h, i] = (f[t][c, core, h, i].astype(F32) + c1[t][c, h, i].astype(F32)).astype(BF16)
                return carry
            lax.fori_loop(0, 4, add, 0)
            for d in (1, 2, 3):
                copy2(t, c, h, d).start()

    def step2(t, c):
        nz = (1, 3)[t]
        for h in range(2):
            for d in (1, 2, 3):
                copy2(t, c, h, d).wait_recv()
            def add(i, carry):
                part = pl.ds(i * nz, nz)
                v = f[t][c, core, h, first[h], part].astype(F32) + c1[t][c, h, first[h], part].astype(F32)
                for d in range(3):
                    v += c2[t][c, h, d, part].astype(F32)
                a2[t][c, h, i] = v.astype(BF16)
                own2[t][i] = v
                return carry
            lax.fori_loop(0, 4, add, 0)
            a3[c, h, pl.ds(t, nz)] = own2[t][second[h]]
            for d in (1, 2, 3):
                copy3(t, c, h, d).start()

    def step3(t, c):
        nz = (1, 3)[t]
        for h in range(2):
            for d in (1, 2, 3):
                copy3(t, c, h, d).wait_recv()
            v = a3[c, h, pl.ds(t, nz)]
            for d in range(3):
                v += c3[t][c, h, d].astype(F32)
            a3[c, h, pl.ds(t, nz)] = v

    def put(n, big, c, v):
        core_of, h, zz = n % 2, n // 2 % 2, n // 4
        one, two = (big // 4, big % 4) if h == 0 else (big % 4, big // 4)
        if zz == 0:
            fa[c, core_of, h, one, two] = v
        else:
            fb[c, core_of, h, one, two * 3 + zz - 1] = v

    wflat[...] = jnp.zeros_like(wflat)
    up[...] = up_t[...].astype(F32).T.astype(BF16)
    def clear(c, carry):
        def one(i, carry):
            for j in range(4):
                fb[c, 1, 1, i, j * 3 + 2] = jnp.zeros((16, 128), BF16)
            return carry
        return lax.fori_loop(0, 4, one, carry)
    lax.fori_loop(0, PIECES, clear, 0)

    def phase_a(c, carry):
        for copy in load(c):
            copy.wait()
        def block(jj, carry):
            here = pl.ds(pl.multiple_of(jj * 256, 256), 256)
            there = pl.ds(pl.multiple_of(c * 2048 + jj * 256, 256), 256)
            gv = gate[c, :, here].astype(F32)
            uv = upp[c, :, here].astype(F32)
            s = 0.5 * jnp.tanh(0.5 * gv) + 0.5
            av = gv * s
            act[:, there] = av
            fac[:, there] = uv * s * (1.0 + gv * (1.0 - s))
            gd = jnp.dot(up_t[...], (av * uv).astype(BF16), preferred_element_type=F32)
            for b in range(2):
                rows[pl.ds(jj * 2 + b, RB, stride=16), :] = gd[:, b * 128 : b * 128 + 128]
            return carry
        lax.fori_loop(0, 8, block, 0, unroll=4)
        def pack(big, carry):
            for idx in range(5):
                at = pl.ds(pl.multiple_of((big * 5 + idx) * 16, 16), 16)
                put(idx if idx < 4 else 14, big, c, rows[at, :].astype(BF16))
            return carry
        lax.fori_loop(0, 16, pack, 0, unroll=2)
        copy1(0, c).start()
        @pl.when(c > 0)
        def _():
            step1(0, c - 1)
        for at, what in ((3, gather_first), (5, lambda: gather_ring(1))):
            @pl.when(c == at)
            def _():
                what()
        return carry

    lax.fori_loop(0, PIECES, phase_a, 0)
    step1(0, PIECES - 1)
    for s in (2, 3, 4):
        gather_ring(s)

    def build(j, carry):
        k = jnp.where(j % 2 == 1, (j + 1) // 2, (8 - j // 2) % 8)
        o = (z + 8 - k) % 8
        for u in range(3):
            copy_y(k, u).wait_recv()
            copy_core(k, mate, u).start()
        for u in range(3):
            copy_core(k, r, u).wait_recv()
            copy_core(k, mate, u).wait_recv()
        for u in range(3):
            off = EV * (8 * u + o) + 4
            for q in range(4):
                for t in range(9 if q < 3 else 6):
                    v = w[o, q, u, t * 16 : t * 16 + 16, :].astype(F32)
                    for half in range(2):
                        at = q * 144 + t * 16 + half * 8
                        if 2 * JIT <= at < 416:
                            wflat[pl.ds(off + at, 8), :] = v[half * 8 : half * 8 + 8]
                        else:
                            wflat[pl.ds(off + at, 8), :] += v[half * 8 : half * 8 + 8]
        return carry

    lax.fori_loop(0, 8, build, 0)

    def phase_b(c, carry):
        def block(jj, carry):
            there = pl.ds(pl.multiple_of(c * 2048 + jj * 256, 256), 256)
            j = c * 16 + jj * 2
            wv = jnp.concatenate(
                [wflat[pl.ds(WPAD + j + b, RB, stride=NB), :] for b in range(2)], axis=1
            ).astype(BF16)
            dh = jnp.dot(up[...], wv, preferred_element_type=F32)
            gg = jnp.dot(tok_t[...], (dh * fac[:, there]).astype(BF16), preferred_element_type=F32)
            gu = jnp.dot(tok_t[...], (dh * act[:, there]).astype(BF16), preferred_element_type=F32)
            for m, v in enumerate((gg, gu)):
                for b in range(2):
                    rows[pl.ds(m * RB * 16 + jj * 2 + b, RB, stride=16), :] = v[:, b * 128 : b * 128 + 128]
            return carry
        lax.fori_loop(0, 8, block, 0, unroll=4)
        def pack(big, carry):
            for n in range(4, 14):
                row = (n - 4) // 5 * RB + (n - 4) % 5
                at = pl.ds(pl.multiple_of((big * 5 + row) * 16, 16), 16)
                put(n, big, c, rows[at, :].astype(BF16))
            return carry
        lax.fori_loop(0, 16, pack, 0, unroll=2)
        copy1(1, c).start()
        step2(0, c)
        @pl.when(c > 0)
        def _():
            step1(1, c - 1)
            step3(0, c - 1)
        return carry

    lax.fori_loop(0, PIECES, phase_b, 0)
    step1(1, PIECES - 1)
    step3(0, PIECES - 1)

    def loop2(c, carry):
        step2(1, c)
        return carry

    def loop3(c, carry):
        step3(1, c)
        for d in range(1, 8):
            copy4(c, d).start()
        return carry

    def loop4(c, carry):
        for d in range(1, 8):
            copy4(c, d).wait_recv()
        v = a3[c, z // 4, z % 4]
        for d in range(7):
            v += c4[c, d]
        g[pl.ds(pl.multiple_of(c * 16, 16), 16), :] = v * (1.0 / 32768.0)
        return carry

    for loop in (loop2, loop3, loop4):
        lax.fori_loop(0, PIECES, loop, 0)

    n_own = member(z, core)
    real = n_own < 15
    own_m = matrix_of(n_own)
    i_own = (x * 4 + y) * 5 + index_of(n_own)
    row = own_m * RB + i_own
    ka, kb = z * 2 + core, x * 4 + y
    in_a = lambda d: (lambda k: device(x, y, k // 2, k % 2))((ka + d) % 16)
    in_b = lambda d: (lambda k: device(k // 4, k % 4, z, core))((kb + d) % 16)

    squares = g[...] * g[...]
    lane = lax.broadcasted_iota(jnp.int32, (1, 128), 1)
    last = jnp.where((lane == i_own) & real, jnp.sum(squares), 0.0) + wext[0:1, :]
    for k in range(16):
        sq[k, 0:7, :] = squares[7 * k : 7 * k + 7, :]
        sq[k, 7:8, :] = last

    def copy_a(d):
        return remote(sq.at[(ka + d) % 16], pa.at[d - 1], ssa.at[d - 1], rsa.at[d - 1], in_a(d))

    def copy_b(d):
        return remote(acc, pb.at[d - 1], ssb.at[d - 1], rsb.at[d - 1], in_b(d))

    def copy_c(d):
        return remote(pc.at[0, z], pc.at[0, z], ssc.at[d - 1], rsc.at[d - 1], along_z(d))

    def copy_d(d):
        return remote(pc.at[0, (z + 8 - d) % 8], pc.at[1, (z + 8 - d) % 8], ssd.at[d], rsd.at[d], other)

    for d in range(1, 16):
        copy_a(d).start()

    gv, qv = row // 15, row % 15

    def give(fn):
        for t in range(6):
            if t < 4:
                owner, k = 4 * gv + t, qv - BASES[t]
                ok = (k >= 0) & (k < COUNTS[t]) & real
                k = jnp.clip(k, 0, 5)
            elif t == 4:
                owner, k, ok = jnp.maximum(4 * gv - 1, 0), 5, (qv == 0) & (gv > 0) & real
            else:
                owner, k, ok = jnp.minimum(4 * gv + 4, 63), 0, (qv == 14) & (gv < 15) & real
            for rr in range(4):
                fn(owner, k, ok, rr, t * 4 + rr)

    def send_row(owner, k, ok, rr, n):
        @pl.when(ok & ((owner != p) | (rr != r)))
        def _():
            remote(g, gw.at[k], ssg.at[n], rsg.at[k], {"rep": rr, "dp": owner}).start()
        @pl.when(ok & (owner == p) & (rr == r))
        def _():
            gw[k] = g[...]

    give(send_row)

    def source(k):
        return matrix_of(member(k // 2, k % 2))

    v = sq[ka]
    for m in range(3):
        acc[m] = jnp.where(own_m == m, v, 0.0)
    for d in range(1, 16):
        copy_a(d).wait_recv()
        v = pa[d - 1]
        m_src = source((ka + 16 - d) % 16)
        for m in range(3):
            acc[m] += jnp.where(m_src == m, v, 0.0)
    for d in range(1, 16):
        copy_b(d).start()
    tot[...] = acc[...]
    for d in range(1, 16):
        copy_b(d).wait_recv()
        tot[...] += pb[d - 1]
    pc[0, z] = tot[...]
    for d in (4, 3, 5, 2, 6, 1, 7):
        copy_c(d).start()
    copy_d(0).start()
    extra[...] = tot[...]
    for d in (1, 7, 2, 6, 3, 5, 4):
        copy_c(d).wait_recv()
        copy_d(d).start()
    for d in range(8):
        copy_d(d).wait_recv()
    for k in range(8):
        for m in range(3):
            cols[m, 2 * k + core] = pc[0, k, m]
            cols[m, 2 * k + 1 - core] = pc[1, k, m]

    a = p % 4
    base = 15 * (p // 4) + jnp.where(a == 0, -1, jnp.where(a == 1, 3, jnp.where(a == 2, 7, 10)))
    for k in range(6):
        if k == 0:
            ok = p > 0
        elif k == 5:
            ok = (a == 0) | ((a == 3) & (p < 63))
        else:
            ok = p >= 0
        @pl.when(ok & ((base + k != row) | jnp.logical_not(real)))
        def _():
            remote(g, gw.at[k], ssg.at[k], rsg.at[k], other).wait_recv()
        @pl.when(jnp.logical_not(ok))
        def _():
            gw[k] = jnp.zeros((NB, 128), F32)

    def wait_row(owner, k, ok, rr, n):
        @pl.when(ok & ((owner != p) | (rr != r)))
        def _():
            remote(g, gw.at[k], ssg.at[n], rsg.at[k], {"rep": rr, "dp": owner}).wait_send()

    give(wait_row)
    for d in range(1, 16):
        copy_a(d).wait_send()
        copy_b(d).wait_send()
    for d in range(8):
        if d:
            copy_c(d).wait_send()
        copy_d(d).wait_send()

    @pl.when(p >= 40)
    def _():
        for d in range(1, 8):
            copy_spread(d).wait_send()

    for u in range(3):
        for s in range(1, 5):
            copy_up(s, u).wait_send()
            if s < 4:
                copy_down(s, u).wait_send()

    def drain_w(k, carry):
        for u in range(3):
            copy_y(k, u).wait_send()
            copy_core(k, r, u).wait_send()
            copy_core(k, mate, u).wait_send()
        return carry

    def drain(c, carry):
        for t in range(2):
            copy1(t, c).wait_send()
            for h in range(2):
                for d in (1, 2, 3):
                    copy2(t, c, h, d).wait_send()
                    copy3(t, c, h, d).wait_send()
        for d in range(1, 8):
            copy4(c, d).wait_send()
        return carry

    lax.fori_loop(0, 8, drain_w, 0)
    lax.fori_loop(0, PIECES, drain, 0)


def main(tokens, upstream, gate_pre, up_pre, quarter, wext):
    n = PIECES
    dma = lambda *shape: pltpu.SemaphoreType.DMA(shape)
    vm = pl.BlockSpec(memory_space=pltpu.VMEM)
    hbm = pl.BlockSpec(memory_space=pl.ANY)
    both = lambda *shape: [pltpu.VMEM(shape[:-1] + (k * shape[-1], 16, 128), BF16) for k in (1, 3)]
    return pl.pallas_call(
        main_kernel,
        in_specs=[vm, vm, hbm, hbm, vm, vm],
        out_specs=[vm, vm, vm],
        out_shape=[
            jax.ShapeDtypeStruct((6, NB, 128), F32),
            jax.ShapeDtypeStruct((3, 16, 8, 128), F32),
            jax.ShapeDtypeStruct((3, 8, 128), F32),
        ],
        scratch_shapes=[
            pltpu.VMEM((n, 128, 2048), BF16),
            pltpu.VMEM((n, 128, 2048), BF16),
            pltpu.VMEM((128, 14336), F32),
            pltpu.VMEM((128, 14336), F32),
            pltpu.VMEM((8, 4, 3, 144, 128), BF16),
            pltpu.VMEM((WROWS, 128), F32),
            pltpu.VMEM((2 * RB * 16, 128), F32),
            *both(n, 2, 2, 4, 4),
            *both(n, 2, 4, 4),
            *both(n, 2, 4, 4),
            *both(n, 2, 3, 4),
            *both(n, 2, 4, 1),
            pltpu.VMEM((4, 1, 16, 128), F32),
            pltpu.VMEM((4, 3, 16, 128), F32),
            *both(n, 2, 3, 1),
            pltpu.VMEM((n, 2, 4, 16, 128), F32),
            pltpu.VMEM((n, 7, 16, 128), F32),
            pltpu.VMEM((128, RB), BF16),
            pltpu.VMEM((NB, 128), F32),
            pltpu.VMEM((16, 8, 128), F32),
            pltpu.VMEM((15, 8, 128), F32),
            pltpu.VMEM((3, 8, 128), F32),
            pltpu.VMEM((15, 3, 8, 128), F32),
            pltpu.VMEM((3, 8, 128), F32),
            pltpu.VMEM((2, 8, 3, 8, 128), F32),
            dma(n), dma(n),
            dma(7), dma(3), dma(12), dma(12), dma(9), dma(9), dma(24), dma(24), dma(48), dma(48),
            dma(2 * n), dma(2 * n), dma(2 * n, 6), dma(2 * n, 6), dma(2 * n, 6), dma(2 * n, 6), dma(n, 7), dma(n, 7),
            dma(15), dma(15), dma(15), dma(15), dma(7), dma(7), dma(8), dma(8), dma(24), dma(6),
        ],
        compiler_params=pltpu.CompilerParams(
            vmem_limit_bytes=VMEM_LIMIT, collective_id=0, has_side_effects=True
        ),
        name="main",
    )(tokens.T, upstream.T, gate_pre, up_pre, quarter, wext)


def update_kernel(lengths, gw, cols, extra, params, row_state, col_state, out_p, out_d, out_r, out_c, moved, scaled):
    p = lax.axis_index("dp")
    start, length = span(lengths)
    a = p % 4
    first = 15 * (p // 4) + jnp.where(a == 0, -1, jnp.where(a == 1, 3, jnp.where(a == 2, 7, 10)))
    shift = start - NB * first
    for m in range(3):
        for k in range(16):
            part = pl.ds(m * NB + 7 * k, 7)
            out_c[part, :] = BETA * col_state[part, :] + (1.0 - BETA) * (cols[m, k, 0:7, :] * (1.0 / RB) + TINY)
    lane = lax.broadcasted_iota(jnp.int32, (1, 128), 1)
    sums_row = extra[:, 7, :]
    live = lax.broadcasted_iota(jnp.int32, (3, 128), 1) < RB
    rows = jnp.where(live, BETA * row_state[...] + (1.0 - BETA) * (sums_row * (1.0 / 14336.0) + TINY), 0.0)
    out_r[...] = rows
    means = jnp.sum(rows, axis=1, keepdims=True) * (1.0 / RB)
    weight = jnp.sum(sums_row, axis=0, keepdims=True)
    for k in range(6):
        row = jnp.clip(first + k, 0, 239)
        m = row // RB
        i = row % RB
        pick = lambda v: jnp.where(m == 0, v[0:1], jnp.where(m == 1, v[1:2], v[2:3]))
        value = jnp.sum(jnp.where(lane == i, pick(rows), 0.0), axis=1, keepdims=True)
        sq = jnp.sum(jnp.where(lane == 120 + m, weight, 0.0), axis=1, keepdims=True)
        scale = RHO * jnp.sqrt(sq * (1.0 / (RB * 14336.0)))
        factor = value / pick(means)
        v = gw[k] * lax.rsqrt(factor * out_c[pl.ds(pl.multiple_of(m * NB, 8), NB), :])
        moved[pl.ds(k * NB, NB), :] = v
        scaled[pl.ds(k * NB, NB), :] = scale * v
    def tile(t, carry):
        o = pl.multiple_of(t * 16, 16)
        at = pl.ds(shift + o, 16)
        keep = o + lax.broadcasted_iota(jnp.int32, (16, 128), 0) < length
        out_d[pl.ds(o, 16), :] = jnp.where(keep, moved[at, :], 0.0).astype(BF16)
        new = params[pl.ds(o, 16), :].astype(F32) - scaled[at, :]
        out_p[pl.ds(o, 16), :] = jnp.where(keep, new, 0.0).astype(BF16)
        return carry
    lax.fori_loop(0, 34, tile, 0)


def update(lengths, gw, cols, extra, params, row_state, col_state):
    vm = pl.BlockSpec(memory_space=pltpu.VMEM)
    return pl.pallas_call(
        update_kernel,
        in_specs=[pl.BlockSpec(memory_space=pltpu.SMEM)] + [vm] * 6,
        out_specs=[vm] * 4,
        out_shape=[
            jax.ShapeDtypeStruct((544, 128), BF16),
            jax.ShapeDtypeStruct((544, 128), BF16),
            jax.ShapeDtypeStruct((3, 128), F32),
            jax.ShapeDtypeStruct((336, 128), F32),
        ],
        scratch_shapes=[pltpu.VMEM((800, 128), F32), pltpu.VMEM((800, 128), F32)],
        compiler_params=pltpu.CompilerParams(vmem_limit_bytes=VMEM_LIMIT),
        name="update",
    )(lengths, gw, cols, extra, params, row_state, col_state)


def body(tokens, upstream, gate_pre, up_pre, param_shards, shard_rows, row_state, col_state):
    quarter, wext = prep(shard_rows, param_shards)
    gw, cols, extra = main(tokens, upstream, gate_pre, up_pre, quarter, wext)
    row_in = jnp.pad(row_state.reshape(3, RB), ((0, 0), (0, 128 - RB)))
    new_params, direction, rows, new_cols = update(
        shard_rows, gw, cols, extra, param_shards, row_in, col_state.reshape(336, 128)
    )
    return (new_params, direction, rows[:, :RB].reshape(-1), new_cols.reshape(-1))


def solution(mesh):
    in_specs = (
        P(("rep", "dp"), None),
        P(("rep", "dp"), None),
        P(("rep", "dp"), None),
        P(("rep", "dp"), None),
        P("dp", None),
        P(),
        P(),
        P(),
    )
    out_specs = (P("dp", None), P("dp", None), P(), P())
    return jax.shard_map(body, mesh=mesh, in_specs=in_specs, out_specs=out_specs, check_vma=False)
```

```python
import functools

import jax
import jax.numpy as jnp
from jax import lax
from jax.experimental import pallas as pl
from jax.experimental.pallas import tpu as pltpu
from jax.sharding import PartitionSpec as P

BETA = 0.8
RHO = 0.2
TINY = 1e-30
RB = 80
NB = 112
EV = 420
JIT = 52
PIECES = 7
WPAD = 1176
WROWS = 10200
BASES = (-1, 3, 7, 10)
COUNTS = (6, 5, 5, 6)
F32 = jnp.float32
BF16 = jnp.bfloat16
VMEM_LIMIT = 60 * 1024 * 1024


def coords():
    r = lax.axis_index("rep")
    p = lax.axis_index("dp")
    x = p // 16
    y = (p // 8 % 2) * 2 + r // 2
    return x, y, p % 8, r % 2


def device(x, y, z, core):
    return {"rep": (y % 2) * 2 + core, "dp": (x * 2 + y // 2) * 8 + z}


def hello(targets):
    barrier = pltpu.get_barrier_semaphore()
    for target in targets:
        pl.semaphore_signal(barrier, inc=1, device_id=target, device_id_type=pl.DeviceIdType.MESH)


def remote(src, dst, send, recv, target):
    return pltpu.make_async_remote_copy(
        src_ref=src, dst_ref=dst, send_sem=send, recv_sem=recv,
        device_id=target, device_id_type=pl.DeviceIdType.MESH,
    )


def span(lengths):
    p = lax.axis_index("dp")
    add = lambda k, total: total + jnp.where(k < p, lengths[k], 0)
    start = lax.fori_loop(0, 64, add, jnp.int32(0), unroll=8)
    return start, lengths[p]


def prep_kernel(lengths, params, quarter, wext, shifted):
    p, r = lax.axis_index("dp"), lax.axis_index("rep")
    start, length = span(lengths)
    row = lax.broadcasted_iota(jnp.int32, (544, 128), 0)
    v = jnp.where(row < length, params[...].astype(F32), 0.0)
    shifted[0 : 2 * JIT, :] = jnp.zeros((2 * JIT, 128), F32)
    shifted[2 * JIT : 2 * JIT + 544, :] = v
    shifted[2 * JIT + 544 :, :] = jnp.zeros((72, 128), F32)
    at = jnp.clip(2 * JIT - (start - (EV * p - JIT)) + 144 * r, 0, 576)
    quarter[...] = shifted[pl.ds(at, 144), :].astype(BF16)
    v = v * v
    flat = row + start
    lane = lax.broadcasted_iota(jnp.int32, (8, 128), 1)
    total = jnp.zeros((8, 128), F32)
    for m in range(3):
        inside = (flat >= m * 8960) & (flat < m * 8960 + 8960)
        total += jnp.where(lane == 120 + m, 0.25 * jnp.sum(jnp.where(inside, v, 0.0)), 0.0)
    wext[...] = total


def prep(shard_rows, params):
    vm = pl.BlockSpec(memory_space=pltpu.VMEM)
    return pl.pallas_call(
        prep_kernel,
        in_specs=[pl.BlockSpec(memory_space=pltpu.SMEM), vm],
        out_specs=[vm, vm],
        out_shape=[jax.ShapeDtypeStruct((144, 128), BF16), jax.ShapeDtypeStruct((8, 128), F32)],
        scratch_shapes=[pltpu.VMEM((720, 128), F32)],
        compiler_params=pltpu.CompilerParams(vmem_limit_bytes=VMEM_LIMIT),
        name="prep",
    )(shard_rows, params)


def matrix_of(n):
    return jnp.where(n < 4, 2, jnp.where(n < 9, 0, jnp.where(n < 14, 1, 2)))


def index_of(n):
    return jnp.where(n < 4, n, jnp.where(n < 9, n - 4, jnp.where(n < 14, n - 9, 4)))


def member(z, core):
    return z % 4 * 4 + z // 4 * 2 + core


def main_kernel(
    tok_t, up_t, gate_hbm, upp_hbm, quarter, wext, gw, cols, extra,
    gate, upp, act, fac, w, wflat, rows, fa, fb, c1a, c1b, a1a, a1b, c2a, c2b, a2a, a2b, own2a, own2b,
    c3a, c3b, a3, c4, up, g, gb, sq, pa, acc, pb, tot, pc,
    sg, su, w1, v1, wp, vp, wm, vm, wy, vy, wc, vc,
    s1, r1, s2, r2, s3, r3, s4, r4, ssa, rsa, ssb, rsb, ssc, rsc, ssd, rsd, ssg, rsg, ssf, rsf,
):
    x, y, z, core = coords()
    r, p = lax.axis_index("rep"), lax.axis_index("dp")
    plane = p // 8
    other = device(x, y, z, 1 - core)
    along_x = lambda d: device((x + d) % 4, y, z, core)
    along_y = lambda d: device(x, (y + d) % 4, z, core)
    along_z = lambda d: device(x, y, (z + d) % 8, core)

    def load(c):
        part = pl.ds(pl.multiple_of(c * 2048, 2048), 2048)
        return (
            pltpu.make_async_copy(gate_hbm.at[:, part], gate.at[c], sg.at[c]),
            pltpu.make_async_copy(upp_hbm.at[:, part], upp.at[c], su.at[c]),
        )

    def begin(c, carry):
        for copy in load(c):
            copy.start()
        return carry

    lax.fori_loop(0, PIECES, begin, 0)
    hello(
        [other]
        + [along_x(d) for d in (1, 2, 3)]
        + [along_y(d) for d in (1, 2, 3)]
        + [along_z(d) for d in range(1, 8)]
        + [device((x + d) % 4, (y + 2) % 4, z, core) for d in (1, 2, 3)]
    )
    pl.semaphore_wait(pltpu.get_barrier_semaphore(), 17)

    spread = lambda d: {"rep": r, "dp": (plane + d) % 8 * 8 + z}
    mate = (1 - r // 2) * 2 + core

    def copy_spread(d):
        return remote(quarter, w.at[z, r, jnp.maximum(plane - 5, 0)], w1.at[d - 1], v1.at[jnp.maximum(plane - 5, 0)], spread(d))

    def copy_up(s, u):
        block = w.at[(z + 9 - s) % 8, r, u]
        n = (s - 1) * 3 + u
        return remote(block, block, wp.at[n], vp.at[n], along_z(1))

    def copy_down(s, u):
        block = w.at[(z + s - 1) % 8, r, u]
        n = (s - 1) * 3 + u
        return remote(block, block, wm.at[n], vm.at[n], along_z(7))

    def copy_y(k, u):
        block = w.at[(z + 8 - k) % 8, r, u]
        to = jnp.where((k == 0) | (k > 4), 3, 1)
        return remote(block, block, wy.at[k * 3 + u], vy.at[k * 3 + u], along_y(to))

    def copy_core(k, q, u):
        block = w.at[(z + 8 - k) % 8, q, u]
        n = (jnp.where(q == r, 0, 8) + k) * 3 + u
        return remote(block, block, wc.at[n], vc.at[n], other)

    @pl.when(p >= 40)
    def _():
        for d in range(1, 8):
            copy_spread(d).start()
        w[z, r, jnp.maximum(plane - 5, 0)] = quarter[...]

    def gather_first():
        for u in range(3):
            @pl.when(plane != 5 + u)
            def _():
                remote(quarter, w.at[z, r, u], w1.at[0], v1.at[u], spread(1)).wait_recv()
            copy_up(1, u).start()
            copy_down(1, u).start()
            copy_y(0, u).start()
            copy_core(0, r, u).start()

    def gather_ring(s):
        for u in range(3):
            copy_up(s, u).wait_recv()
            if s < 4:
                copy_up(s + 1, u).start()
            copy_y(s, u).start()
            copy_core(s, r, u).start()
            if s < 4:
                copy_down(s, u).wait_recv()
                if s < 3:
                    copy_down(s + 1, u).start()
                copy_y(8 - s, u).start()
                copy_core(8 - s, r, u).start()

    f, c1, a1, c2 = (fa, fb), (c1a, c1b), (a1a, a1b), (c2a, c2b)
    a2, own2, c3 = (a2a, a2b), (own2a, own2b), (c3a, c3b)
    first, second = (x, y), (y, x)
    axis_of = (along_x, along_y)

    def copy1(t, c):
        k = t * PIECES + c
        return remote(f[t].at[c, 1 - core], c1[t].at[c], s1.at[k], r1.at[k], other)

    def copy2(t, c, h, d):
        k, n = t * PIECES + c, h * 3 + d - 1
        return remote(a1[t].at[c, h, (first[h] + d) % 4], c2[t].at[c, h, d - 1], s2.at[k, n], r2.at[k, n], axis_of[h](d))

    def copy3(t, c, h, d):
        k, n = t * PIECES + c, h * 3 + d - 1
        return remote(a2[t].at[c, h, (second[h] + d) % 4], c3[t].at[c, h, d - 1], s3.at[k, n], r3.at[k, n], axis_of[1 - h](d))

    def copy4(c, d):
        to = (z + d) % 8
        return remote(a3.at[c, to // 4, to % 4], c4.at[c, d - 1], s4.at[c, d - 1], r4.at[c, d - 1], along_z(d))

    def step1(t, c):
        copy1(t, c).wait_recv()
        for h in range(2):
            def add(i, carry):
                a1[t][c, h, i] = (f[t][c, core, h, i].astype(F32) + c1[t][c, h, i].astype(F32)).astype(BF16)
                return carry
            lax.fori_loop(0, 4, add, 0)
            for d in (1, 2, 3):
                copy2(t, c, h, d).start()

    def step2(t, c):
        nz = (1, 3)[t]
        for h in range(2):
            for d in (1, 2, 3):
                copy2(t, c, h, d).wait_recv()
            def add(i, carry):
                part = pl.ds(i * nz, nz)
                v = f[t][c, core, h, first[h], part].astype(F32) + c1[t][c, h, first[h], part].astype(F32)
                for d in range(3):
                    v += c2[t][c, h, d, part].astype(F32)
                a2[t][c, h, i] = v.astype(BF16)
                own2[t][i] = v
                return carry
            lax.fori_loop(0, 4, add, 0)
            a3[c, h, pl.ds(t, nz)] = own2[t][second[h]]
            for d in (1, 2, 3):
                copy3(t, c, h, d).start()

    def step3(t, c):
        nz = (1, 3)[t]
        for h in range(2):
            for d in (1, 2, 3):
                copy3(t, c, h, d).wait_recv()
            v = a3[c, h, pl.ds(t, nz)]
            for d in range(3):
                v += c3[t][c, h, d].astype(F32)
            a3[c, h, pl.ds(t, nz)] = v

    def put(n, big, c, v):
        core_of, h, zz = n % 2, n // 2 % 2, n // 4
        one, two = (big // 4, big % 4) if h == 0 else (big % 4, big // 4)
        if zz == 0:
            fa[c, core_of, h, one, two] = v
        else:
            fb[c, core_of, h, one, two * 3 + zz - 1] = v

    wflat[...] = jnp.zeros_like(wflat)
    up[...] = up_t[...].astype(F32).T.astype(BF16)
    def clear(c, carry):
        def one(i, carry):
            for j in range(4):
                fb[c, 1, 1, i, j * 3 + 2] = jnp.zeros((16, 128), BF16)
            return carry
        return lax.fori_loop(0, 4, one, carry)
    lax.fori_loop(0, PIECES, clear, 0)

    def phase_a(c, carry):
        for copy in load(c):
            copy.wait()
        def block(jj, carry):
            here = pl.ds(pl.multiple_of(jj * 256, 256), 256)
            there = pl.ds(pl.multiple_of(c * 2048 + jj * 256, 256), 256)
            gv = gate[c, :, here].astype(F32)
            uv = upp[c, :, here].astype(F32)
            s = 0.5 * jnp.tanh(0.5 * gv) + 0.5
            av = gv * s
            act[:, there] = av
            fac[:, there] = uv * s * (1.0 + gv * (1.0 - s))
            gd = jnp.dot(up_t[...], (av * uv).astype(BF16), preferred_element_type=F32)
            for b in range(2):
                rows[pl.ds(jj * 2 + b, RB, stride=16), :] = gd[:, b * 128 : b * 128 + 128]
            return carry
        lax.fori_loop(0, 8, block, 0, unroll=4)
        def pack(big, carry):
            for idx in range(5):
                at = pl.ds(pl.multiple_of((big * 5 + idx) * 16, 16), 16)
                put(idx if idx < 4 else 14, big, c, rows[at, :].astype(BF16))
            return carry
        lax.fori_loop(0, 16, pack, 0, unroll=2)
        copy1(0, c).start()
        @pl.when(c > 0)
        def _():
            step1(0, c - 1)
        for at, what in ((2, gather_first), (3, lambda: gather_ring(1)), (5, lambda: gather_ring(2))):
            @pl.when(c == at)
            def _():
                what()
        return carry

    lax.fori_loop(0, PIECES, phase_a, 0)
    step1(0, PIECES - 1)
    gather_ring(3)
    for c in range(4):
        step2(0, c)
    gather_ring(4)
    for c in range(4, PIECES):
        step2(0, c)

    def build(j, carry):
        k = jnp.where(j % 2 == 1, (j + 1) // 2, (8 - j // 2) % 8)
        o = (z + 8 - k) % 8
        for u in range(3):
            copy_y(k, u).wait_recv()
            copy_core(k, mate, u).start()
        for u in range(3):
            copy_core(k, r, u).wait_recv()
            copy_core(k, mate, u).wait_recv()
        for u in range(3):
            off = EV * (8 * u + o) + 4
            for q in range(4):
                for t in range(9 if q < 3 else 6):
                    v = w[o, q, u, t * 16 : t * 16 + 16, :].astype(F32)
                    for half in range(2):
                        at = q * 144 + t * 16 + half * 8
                        if 2 * JIT <= at < 416:
                            wflat[pl.ds(off + at, 8), :] = v[half * 8 : half * 8 + 8]
                        else:
                            wflat[pl.ds(off + at, 8), :] += v[half * 8 : half * 8 + 8]
        return carry

    lax.fori_loop(0, 8, build, 0)

    def phase_b(c, carry):
        def block(jj, carry):
            there = pl.ds(pl.multiple_of(c * 2048 + jj * 256, 256), 256)
            j = c * 16 + jj * 2
            wv = jnp.concatenate(
                [wflat[pl.ds(WPAD + j + b, RB, stride=NB), :] for b in range(2)], axis=1
            ).astype(BF16)
            dh = jnp.dot(up[...], wv, preferred_element_type=F32)
            gg = jnp.dot(tok_t[...], (dh * fac[:, there]).astype(BF16), preferred_element_type=F32)
            gu = jnp.dot(tok_t[...], (dh * act[:, there]).astype(BF16), preferred_element_type=F32)
            for m, v in enumerate((gg, gu)):
                for b in range(2):
                    rows[pl.ds(m * RB * 16 + jj * 2 + b, RB, stride=16), :] = v[:, b * 128 : b * 128 + 128]
            return carry
        lax.fori_loop(0, 8, block, 0, unroll=4)
        def pack(big, carry):
            for n in range(4, 14):
                row = (n - 4) // 5 * RB + (n - 4) % 5
                at = pl.ds(pl.multiple_of((big * 5 + row) * 16, 16), 16)
                put(n, big, c, rows[at, :].astype(BF16))
            return carry
        lax.fori_loop(0, 16, pack, 0, unroll=2)
        copy1(1, c).start()
        step3(0, c)
        @pl.when(c > 0)
        def _():
            step1(1, c - 1)
        @pl.when(c > 2)
        def _():
            step2(1, c - 3)
        @pl.when(c > 3)
        def _():
            last_two(c - 4)
        return carry

    def last_two(c):
        step3(1, c)
        for d in range(1, 8):
            copy4(c, d).start()

    lax.fori_loop(0, PIECES, phase_b, 0)
    step1(1, PIECES - 1)

    for c in range(PIECES - 3, PIECES):
        step2(1, c)
        last_two(c - 1)
    last_two(PIECES - 1)

    def loop4(c, carry):
        for d in range(1, 8):
            copy4(c, d).wait_recv()
        v = a3[c, z // 4, z % 4]
        for d in range(7):
            v += c4[c, d]
        g[pl.ds(pl.multiple_of(c * 16, 16), 16), :] = v * (1.0 / 32768.0)
        return carry

    lax.fori_loop(0, PIECES, loop4, 0)

    n_own = member(z, core)
    real = n_own < 15
    own_m = matrix_of(n_own)
    i_own = (x * 4 + y) * 5 + index_of(n_own)
    row = own_m * RB + i_own
    ka, kb = z * 2 + core, x * 4 + y
    in_a = lambda d: (lambda k: device(x, y, k // 2, k % 2))((ka + d) % 16)
    in_b = lambda d: (lambda k: device(k // 4, k % 4, z, core))((kb + d) % 16)

    squares = g[...] * g[...]
    lane = lax.broadcasted_iota(jnp.int32, (1, 128), 1)
    last = jnp.where((lane == i_own) & real, jnp.sum(squares), 0.0) + wext[0:1, :]
    for k in range(16):
        sq[k, 0:7, :] = squares[7 * k : 7 * k + 7, :]
        sq[k, 7:8, :] = last

    def copy_a(d):
        return remote(sq.at[(ka + d) % 16], pa.at[d - 1], ssa.at[d - 1], rsa.at[d - 1], in_a(d))

    def copy_b(d):
        return remote(acc, pb.at[d - 1], ssb.at[d - 1], rsb.at[d - 1], in_b(d))

    def copy_c(d):
        return remote(pc.at[0, z], pc.at[0, z], ssc.at[d - 1], rsc.at[d - 1], along_z(d))

    def copy_d(d):
        return remote(pc.at[0, (z + 8 - d) % 8], pc.at[1, (z + 8 - d) % 8], ssd.at[d], rsd.at[d], other)

    for d in range(1, 16):
        copy_a(d).start()

    gv, qv = row // 15, row % 15

    def give(fn):
        for t in range(6):
            if t < 4:
                owner, k = 4 * gv + t, qv - BASES[t]
                ok = (k >= 0) & (k < COUNTS[t]) & real
                k = jnp.clip(k, 0, 5)
            elif t == 4:
                owner, k, ok = jnp.maximum(4 * gv - 1, 0), 5, (qv == 0) & (gv > 0) & real
            else:
                owner, k, ok = jnp.minimum(4 * gv + 4, 63), 0, (qv == 14) & (gv < 15) & real
            for half in range(2):
                fn(owner, k, ok, 2 * half + core, t * 2 + half)

    def send_row(owner, k, ok, rr, n):
        @pl.when(ok & ((owner != p) | (rr != r)))
        def _():
            remote(gb, gw.at[k], ssg.at[n], rsg.at[k], {"rep": rr, "dp": owner}).start()
        @pl.when(ok & (owner == p) & (rr == r))
        def _():
            gw[k] = gb[...]

    gb[...] = g[...].astype(BF16)
    give(send_row)

    a = p % 4
    base = 15 * (p // 4) + jnp.where(a == 0, -1, jnp.where(a == 1, 3, jnp.where(a == 2, 7, 10)))

    def window(arriving):
        for k in range(6):
            if k == 0:
                ok = p > 0
            elif k == 5:
                ok = (a == 0) | ((a == 3) & (p < 63))
            else:
                ok = p >= 0
            at = jnp.clip(base + k, 0, 239)
            m, idx = at // RB, at % 5
            from_core = jnp.where(m == 2, jnp.where(idx < 4, idx, 14), jnp.where(m == 0, 4 + idx, 9 + idx)) % 2
            hand = remote(gw.at[k], gw.at[k], ssf.at[k], rsf.at[k], other)
            if arriving:
                @pl.when(ok & (from_core == core) & ((base + k != row) | jnp.logical_not(real)))
                def _():
                    remote(gb, gw.at[k], ssg.at[k], rsg.at[k], other).wait_recv()
                @pl.when(ok & (from_core == core))
                def _():
                    hand.start()
                @pl.when(jnp.logical_not(ok))
                def _():
                    gw[k] = jnp.zeros((NB, 128), BF16)
            else:
                @pl.when(ok & (from_core != core))
                def _():
                    hand.wait_recv()
                @pl.when(ok & (from_core == core))
                def _():
                    hand.wait_send()

    def source(k):
        return matrix_of(member(k // 2, k % 2))

    v = sq[ka]
    for m in range(3):
        acc[m] = jnp.where(own_m == m, v, 0.0)
    for d in range(1, 16):
        copy_a(d).wait_recv()
        v = pa[d - 1]
        m_src = source((ka + 16 - d) % 16)
        for m in range(3):
            acc[m] += jnp.where(m_src == m, v, 0.0)
    for d in range(1, 16):
        copy_b(d).start()
    tot[...] = acc[...]
    for d in range(1, 16):
        copy_b(d).wait_recv()
        tot[...] += pb[d - 1]
    pc[0, z] = tot[...]
    for d in (4, 3, 5, 2, 6, 1, 7):
        copy_c(d).start()
    copy_d(0).start()
    extra[...] = tot[...]
    window(True)
    for d in (1, 7, 2, 6, 3, 5, 4):
        copy_c(d).wait_recv()
        copy_d(d).start()
    for d in range(8):
        copy_d(d).wait_recv()
    window(False)
    for k in range(8):
        for m in range(3):
            cols[m, 2 * k + core] = pc[0, k, m]
            cols[m, 2 * k + 1 - core] = pc[1, k, m]

    def wait_row(owner, k, ok, rr, n):
        @pl.when(ok & ((owner != p) | (rr != r)))
        def _():
            remote(gb, gw.at[k], ssg.at[n], rsg.at[k], {"rep": rr, "dp": owner}).wait_send()

    give(wait_row)
    for d in range(1, 16):
        copy_a(d).wait_send()
        copy_b(d).wait_send()
    for d in range(8):
        if d:
            copy_c(d).wait_send()
        copy_d(d).wait_send()

    @pl.when(p >= 40)
    def _():
        for d in range(1, 8):
            copy_spread(d).wait_send()

    for u in range(3):
        for s in range(1, 5):
            copy_up(s, u).wait_send()
            if s < 4:
                copy_down(s, u).wait_send()

    def drain_w(k, carry):
        for u in range(3):
            copy_y(k, u).wait_send()
            copy_core(k, r, u).wait_send()
            copy_core(k, mate, u).wait_send()
        return carry

    def drain(c, carry):
        for t in range(2):
            copy1(t, c).wait_send()
            for h in range(2):
                for d in (1, 2, 3):
                    copy2(t, c, h, d).wait_send()
                    copy3(t, c, h, d).wait_send()
        for d in range(1, 8):
            copy4(c, d).wait_send()
        return carry

    lax.fori_loop(0, 8, drain_w, 0)
    lax.fori_loop(0, PIECES, drain, 0)


def main(tokens, upstream, gate_pre, up_pre, quarter, wext):
    n = PIECES
    dma = lambda *shape: pltpu.SemaphoreType.DMA(shape)
    vm = pl.BlockSpec(memory_space=pltpu.VMEM)
    hbm = pl.BlockSpec(memory_space=pl.ANY)
    both = lambda *shape: [pltpu.VMEM(shape[:-1] + (k * shape[-1], 16, 128), BF16) for k in (1, 3)]
    return pl.pallas_call(
        main_kernel,
        in_specs=[vm, vm, hbm, hbm, vm, vm],
        out_specs=[vm, vm, vm],
        out_shape=[
            jax.ShapeDtypeStruct((6, NB, 128), BF16),
            jax.ShapeDtypeStruct((3, 16, 8, 128), F32),
            jax.ShapeDtypeStruct((3, 8, 128), F32),
        ],
        scratch_shapes=[
            pltpu.VMEM((n, 128, 2048), BF16),
            pltpu.VMEM((n, 128, 2048), BF16),
            pltpu.VMEM((128, 14336), F32),
            pltpu.VMEM((128, 14336), F32),
            pltpu.VMEM((8, 4, 3, 144, 128), BF16),
            pltpu.VMEM((WROWS, 128), F32),
            pltpu.VMEM((2 * RB * 16, 128), F32),
            *both(n, 2, 2, 4, 4),
            *both(n, 2, 4, 4),
            *both(n, 2, 4, 4),
            *both(n, 2, 3, 4),
            *both(n, 2, 4, 1),
            pltpu.VMEM((4, 1, 16, 128), F32),
            pltpu.VMEM((4, 3, 16, 128), F32),
            *both(n, 2, 3, 1),
            pltpu.VMEM((n, 2, 4, 16, 128), F32),
            pltpu.VMEM((n, 7, 16, 128), F32),
            pltpu.VMEM((128, RB), BF16),
            pltpu.VMEM((NB, 128), F32),
            pltpu.VMEM((NB, 128), BF16),
            pltpu.VMEM((16, 8, 128), F32),
            pltpu.VMEM((15, 8, 128), F32),
            pltpu.VMEM((3, 8, 128), F32),
            pltpu.VMEM((15, 3, 8, 128), F32),
            pltpu.VMEM((3, 8, 128), F32),
            pltpu.VMEM((2, 8, 3, 8, 128), F32),
            dma(n), dma(n),
            dma(7), dma(3), dma(12), dma(12), dma(9), dma(9), dma(24), dma(24), dma(48), dma(48),
            dma(2 * n), dma(2 * n), dma(2 * n, 6), dma(2 * n, 6), dma(2 * n, 6), dma(2 * n, 6), dma(n, 7), dma(n, 7),
            dma(15), dma(15), dma(15), dma(15), dma(7), dma(7), dma(8), dma(8), dma(12), dma(6), dma(6), dma(6),
        ],
        compiler_params=pltpu.CompilerParams(
            vmem_limit_bytes=VMEM_LIMIT, collective_id=0, has_side_effects=True
        ),
        name="main",
    )(tokens.T, upstream.T, gate_pre, up_pre, quarter, wext)


def update_kernel(lengths, gw, cols, extra, params, row_state, col_state, out_p, out_d, out_r, out_c, moved, scaled, held):
    p = lax.axis_index("dp")
    start, length = span(lengths)
    a = p % 4
    first = 15 * (p // 4) + jnp.where(a == 0, -1, jnp.where(a == 1, 3, jnp.where(a == 2, 7, 10)))
    shift = start - NB * first
    for m in range(3):
        for k in range(16):
            part = pl.ds(m * NB + 7 * k, 7)
            out_c[part, :] = BETA * col_state[part, :] + (1.0 - BETA) * (cols[m, k, 0:7, :] * (1.0 / RB) + TINY)
    lane = lax.broadcasted_iota(jnp.int32, (1, 128), 1)
    sums_row = extra[:, 7, :]
    live = lax.broadcasted_iota(jnp.int32, (3, 128), 1) < RB
    for m in range(3):
        held[m : m + 1, 0:RB] = row_state[:, m * RB : m * RB + RB]
    rows = jnp.where(live, BETA * held[...] + (1.0 - BETA) * (sums_row * (1.0 / 14336.0) + TINY), 0.0)
    for m in range(3):
        out_r[:, m * RB : m * RB + RB] = rows[m : m + 1, 0:RB]
    means = jnp.sum(rows, axis=1, keepdims=True) * (1.0 / RB)
    weight = jnp.sum(sums_row, axis=0, keepdims=True)
    for k in range(6):
        row = jnp.clip(first + k, 0, 239)
        m = row // RB
        i = row % RB
        pick = lambda v: jnp.where(m == 0, v[0:1], jnp.where(m == 1, v[1:2], v[2:3]))
        value = jnp.sum(jnp.where(lane == i, pick(rows), 0.0), axis=1, keepdims=True)
        sq = jnp.sum(jnp.where(lane == 120 + m, weight, 0.0), axis=1, keepdims=True)
        scale = RHO * jnp.sqrt(sq * (1.0 / (RB * 14336.0)))
        factor = value / pick(means)
        v = gw[k].astype(F32) * lax.rsqrt(factor * out_c[pl.ds(pl.multiple_of(m * NB, 8), NB), :])
        moved[pl.ds(k * NB, NB), :] = v
        scaled[pl.ds(k * NB, NB), :] = scale * v
    def tile(t, carry):
        o = pl.multiple_of(t * 16, 16)
        at = pl.ds(shift + o, 16)
        keep = o + lax.broadcasted_iota(jnp.int32, (16, 128), 0) < length
        out_d[pl.ds(o, 16), :] = jnp.where(keep, moved[at, :], 0.0).astype(BF16)
        new = params[pl.ds(o, 16), :].astype(F32) - scaled[at, :]
        out_p[pl.ds(o, 16), :] = jnp.where(keep, new, 0.0).astype(BF16)
        return carry
    lax.fori_loop(0, 34, tile, 0)


def update(lengths, gw, cols, extra, params, row_state, col_state):
    vm = pl.BlockSpec(memory_space=pltpu.VMEM)
    return pl.pallas_call(
        update_kernel,
        in_specs=[pl.BlockSpec(memory_space=pltpu.SMEM)] + [vm] * 6,
        out_specs=[vm] * 4,
        out_shape=[
            jax.ShapeDtypeStruct((544, 128), BF16),
            jax.ShapeDtypeStruct((544, 128), BF16),
            jax.ShapeDtypeStruct((1, 240), F32),
            jax.ShapeDtypeStruct((336, 128), F32),
        ],
        scratch_shapes=[pltpu.VMEM((800, 128), F32), pltpu.VMEM((800, 128), F32), pltpu.VMEM((3, 128), F32)],
        compiler_params=pltpu.CompilerParams(vmem_limit_bytes=VMEM_LIMIT),
        name="update",
    )(lengths, gw, cols, extra, params, row_state, col_state)


def body(tokens, upstream, gate_pre, up_pre, param_shards, shard_rows, row_state, col_state):
    quarter, wext = prep(shard_rows, param_shards)
    gw, cols, extra = main(tokens, upstream, gate_pre, up_pre, quarter, wext)
    new_params, direction, rows, new_cols = update(
        shard_rows, gw, cols, extra, param_shards, row_state.reshape(1, 240), col_state.reshape(336, 128)
    )
    return (new_params, direction, rows.reshape(-1), new_cols.reshape(-1))


def solution(mesh):
    in_specs = (
        P(("rep", "dp"), None),
        P(("rep", "dp"), None),
        P(("rep", "dp"), None),
        P(("rep", "dp"), None),
        P("dp", None),
        P(),
        P(),
        P(),
    )
    out_specs = (P("dp", None), P("dp", None), P(), P())
    return jax.shard_map(body, mesh=mesh, in_specs=in_specs, out_specs=out_specs, check_vma=False)
```

```python
import functools

import jax
import jax.numpy as jnp
from jax import lax
from jax.experimental import pallas as pl
from jax.experimental.pallas import tpu as pltpu
from jax.sharding import PartitionSpec as P

BETA = 0.8
RHO = 0.2
TINY = 1e-30
RB = 80
NB = 112
EV = 420
JIT = 52
PIECES = 7
WPAD = 1176
WROWS = 10200
BASES = (-1, 3, 7, 10)
COUNTS = (6, 5, 5, 6)
F32 = jnp.float32
BF16 = jnp.bfloat16
VMEM_LIMIT = 60 * 1024 * 1024


def coords():
    r = lax.axis_index("rep")
    p = lax.axis_index("dp")
    x = p // 16
    y = (p // 8 % 2) * 2 + r // 2
    return x, y, p % 8, r % 2


def device(x, y, z, core):
    return {"rep": (y % 2) * 2 + core, "dp": (x * 2 + y // 2) * 8 + z}


def hello(targets):
    barrier = pltpu.get_barrier_semaphore()
    for target in targets:
        pl.semaphore_signal(barrier, inc=1, device_id=target, device_id_type=pl.DeviceIdType.MESH)


def remote(src, dst, send, recv, target):
    return pltpu.make_async_remote_copy(
        src_ref=src, dst_ref=dst, send_sem=send, recv_sem=recv,
        device_id=target, device_id_type=pl.DeviceIdType.MESH,
    )


def span(lengths):
    p = lax.axis_index("dp")
    add = lambda k, total: total + jnp.where(k < p, lengths[k], 0)
    start = lax.fori_loop(0, 64, add, jnp.int32(0), unroll=8)
    return start, lengths[p]


def prep_kernel(lengths, params, quarter, wext, shifted):
    p, r = lax.axis_index("dp"), lax.axis_index("rep")
    start, length = span(lengths)
    row = lax.broadcasted_iota(jnp.int32, (544, 128), 0)
    v = jnp.where(row < length, params[...].astype(F32), 0.0)
    shifted[0 : 2 * JIT, :] = jnp.zeros((2 * JIT, 128), F32)
    shifted[2 * JIT : 2 * JIT + 544, :] = v
    shifted[2 * JIT + 544 :, :] = jnp.zeros((72, 128), F32)
    at = jnp.clip(2 * JIT - (start - (EV * p - JIT)) + 144 * r, 0, 576)
    quarter[...] = shifted[pl.ds(at, 144), :].astype(BF16)
    v = v * v
    flat = row + start
    lane = lax.broadcasted_iota(jnp.int32, (8, 128), 1)
    total = jnp.zeros((8, 128), F32)
    for m in range(3):
        inside = (flat >= m * 8960) & (flat < m * 8960 + 8960)
        total += jnp.where(lane == 120 + m, 0.25 * jnp.sum(jnp.where(inside, v, 0.0)), 0.0)
    wext[...] = total


def prep(shard_rows, params):
    vm = pl.BlockSpec(memory_space=pltpu.VMEM)
    return pl.pallas_call(
        prep_kernel,
        in_specs=[pl.BlockSpec(memory_space=pltpu.SMEM), vm],
        out_specs=[vm, vm],
        out_shape=[jax.ShapeDtypeStruct((144, 128), BF16), jax.ShapeDtypeStruct((8, 128), F32)],
        scratch_shapes=[pltpu.VMEM((720, 128), F32)],
        compiler_params=pltpu.CompilerParams(vmem_limit_bytes=VMEM_LIMIT),
        name="prep",
    )(shard_rows, params)


def matrix_of(n):
    return jnp.where(n < 4, 2, jnp.where(n < 9, 0, jnp.where(n < 14, 1, 2)))


def index_of(n):
    return jnp.where(n < 4, n, jnp.where(n < 9, n - 4, jnp.where(n < 14, n - 9, 4)))


def member(z, core):
    return z % 4 * 4 + z // 4 * 2 + core


def main_kernel(
    tok_t, up_t, gate_hbm, upp_hbm, quarter, wext, gw, cols, extra,
    gate, upp, act, fac, w, wflat, rows, fa, fb, c1a, c1b, a1a, a1b, c2a, c2b, a2a, a2b, own2a, own2b,
    c3a, c3b, a3, c4, up, g, gb, sq, pa, acc, pb, tot, pc,
    sg, su, w1, v1, wp, vp, wm, vm, wy, vy, wc, vc,
    s1, r1, s2, r2, s3, r3, s4, r4, ssa, rsa, ssb, rsb, ssc, rsc, ssd, rsd, ssg, rsg, ssf, rsf,
):
    x, y, z, core = coords()
    r, p = lax.axis_index("rep"), lax.axis_index("dp")
    plane = p // 8
    other = device(x, y, z, 1 - core)
    along_x = lambda d: device((x + d) % 4, y, z, core)
    along_y = lambda d: device(x, (y + d) % 4, z, core)
    along_z = lambda d: device(x, y, (z + d) % 8, core)

    def load(c):
        part = pl.ds(pl.multiple_of(c * 2048, 2048), 2048)
        return (
            pltpu.make_async_copy(gate_hbm.at[:, part], gate.at[c], sg.at[c]),
            pltpu.make_async_copy(upp_hbm.at[:, part], upp.at[c], su.at[c]),
        )

    def begin(c, carry):
        for copy in load(c):
            copy.start()
        return carry

    lax.fori_loop(0, PIECES, begin, 0)
    hello(
        [other]
        + [along_x(d) for d in (1, 2, 3)]
        + [along_y(d) for d in (1, 2, 3)]
        + [along_z(d) for d in range(1, 8)]
        + [device((x + d) % 4, (y + 2) % 4, z, core) for d in (1, 2, 3)]
    )
    pl.semaphore_wait(pltpu.get_barrier_semaphore(), 17)

    spread = lambda d: {"rep": r, "dp": (plane + d) % 8 * 8 + z}
    mate = (1 - r // 2) * 2 + core

    def copy_spread(d):
        return remote(quarter, w.at[z, r, jnp.maximum(plane - 5, 0)], w1.at[d - 1], v1.at[jnp.maximum(plane - 5, 0)], spread(d))

    def copy_up(s, u):
        block = w.at[(z + 9 - s) % 8, r, u]
        n = (s - 1) * 3 + u
        return remote(block, block, wp.at[n], vp.at[n], along_z(1))

    def copy_down(s, u):
        block = w.at[(z + s - 1) % 8, r, u]
        n = (s - 1) * 3 + u
        return remote(block, block, wm.at[n], vm.at[n], along_z(7))

    def copy_y(k, u):
        block = w.at[(z + 8 - k) % 8, r, u]
        to = jnp.where((k == 0) | (k > 4), 3, 1)
        return remote(block, block, wy.at[k * 3 + u], vy.at[k * 3 + u], along_y(to))

    def copy_core(k, q, u):
        block = w.at[(z + 8 - k) % 8, q, u]
        n = (jnp.where(q == r, 0, 8) + k) * 3 + u
        return remote(block, block, wc.at[n], vc.at[n], other)

    @pl.when(p >= 40)
    def _():
        for d in range(1, 8):
            copy_spread(d).start()
        w[z, r, jnp.maximum(plane - 5, 0)] = quarter[...]

    def gather_first():
        for u in range(3):
            @pl.when(plane != 5 + u)
            def _():
                remote(quarter, w.at[z, r, u], w1.at[0], v1.at[u], spread(1)).wait_recv()
            copy_up(1, u).start()
            copy_down(1, u).start()
        for u in range(3):
            copy_y(0, u).start()
        for u in range(3):
            copy_core(0, r, u).start()

    def gather_ring(s):
        for u in range(3):
            for copy, last in ((copy_up, u < 2), (copy_down, u == 2)):
                if s < 4 or last:
                    copy(s, u).wait_recv()
                if s < 3 or (s == 3 and last):
                    copy(s + 1, u).start()
        for u in range(3):
            copy_y(s, u).start()
            if s < 4:
                copy_y(8 - s, u).start()
        for u in range(3):
            copy_core(s, r, u).start()
            if s < 4:
                copy_core(8 - s, r, u).start()
        hand_over(s - 1)
        if s > 1:
            hand_over(9 - s)

    def hand_over(k):
        for u in range(3):
            copy_y(k, u).wait_recv()
            copy_core(k, mate, u).start()

    f, c1, a1, c2 = (fa, fb), (c1a, c1b), (a1a, a1b), (c2a, c2b)
    a2, own2, c3 = (a2a, a2b), (own2a, own2b), (c3a, c3b)
    first, second = (x, y), (y, x)
    axis_of = (along_x, along_y)

    def copy1(t, c):
        k = t * PIECES + c
        return remote(f[t].at[c, 1 - core], c1[t].at[c], s1.at[k], r1.at[k], other)

    def copy2(t, c, h, d):
        k, n = t * PIECES + c, h * 3 + d - 1
        return remote(a1[t].at[c, h, (first[h] + d) % 4], c2[t].at[c, h, d - 1], s2.at[k, n], r2.at[k, n], axis_of[h](d))

    def copy3(t, c, h, d):
        k, n = t * PIECES + c, h * 3 + d - 1
        return remote(a2[t].at[c, h, (second[h] + d) % 4], c3[t].at[c, h, d - 1], s3.at[k, n], r3.at[k, n], axis_of[1 - h](d))

    def copy4(c, d):
        to = (z + d) % 8
        return remote(a3.at[c, to // 4, to % 4], c4.at[c, d - 1], s4.at[c, d - 1], r4.at[c, d - 1], along_z(d))

    def step1(t, c):
        copy1(t, c).wait_recv()
        for h in range(2):
            def add(i, carry):
                a1[t][c, h, i] = (f[t][c, core, h, i].astype(F32) + c1[t][c, h, i].astype(F32)).astype(BF16)
                return carry
            lax.fori_loop(0, 4, add, 0)
            for d in (1, 2, 3):
                copy2(t, c, h, d).start()

    def step2(t, c):
        nz = (1, 3)[t]
        for h in range(2):
            for d in (1, 2, 3):
                copy2(t, c, h, d).wait_recv()
            def add(i, carry):
                part = pl.ds(i * nz, nz)
                v = f[t][c, core, h, first[h], part].astype(F32) + c1[t][c, h, first[h], part].astype(F32)
                for d in range(3):
                    v += c2[t][c, h, d, part].astype(F32)
                a2[t][c, h, i] = v.astype(BF16)
                own2[t][i] = v
                return carry
            lax.fori_loop(0, 4, add, 0)
            a3[c, h, pl.ds(t, nz)] = own2[t][second[h]]
            for d in (1, 2, 3):
                copy3(t, c, h, d).start()

    def step3(t, c):
        nz = (1, 3)[t]
        for h in range(2):
            for d in (1, 2, 3):
                copy3(t, c, h, d).wait_recv()
            v = a3[c, h, pl.ds(t, nz)]
            for d in range(3):
                v += c3[t][c, h, d].astype(F32)
            a3[c, h, pl.ds(t, nz)] = v

    def put(n, big, c, v):
        core_of, h, zz = n % 2, n // 2 % 2, n // 4
        one, two = (big // 4, big % 4) if h == 0 else (big % 4, big // 4)
        if zz == 0:
            fa[c, core_of, h, one, two] = v
        else:
            fb[c, core_of, h, one, two * 3 + zz - 1] = v

    wflat[...] = jnp.zeros_like(wflat)
    up[...] = up_t[...].astype(F32).T.astype(BF16)
    def clear(c, carry):
        def one(i, carry):
            for j in range(4):
                fb[c, 1, 1, i, j * 3 + 2] = jnp.zeros((16, 128), BF16)
            return carry
        return lax.fori_loop(0, 4, one, carry)
    lax.fori_loop(0, PIECES, clear, 0)

    def phase_a(c, carry):
        for copy in load(c):
            copy.wait()
        def block(jj, carry):
            here = pl.ds(pl.multiple_of(jj * 256, 256), 256)
            there = pl.ds(pl.multiple_of(c * 2048 + jj * 256, 256), 256)
            gv = gate[c, :, here].astype(F32)
            uv = upp[c, :, here].astype(F32)
            s = 0.5 * jnp.tanh(0.5 * gv) + 0.5
            av = gv * s
            act[:, there] = av
            fac[:, there] = uv * s * (1.0 + gv * (1.0 - s))
            gd = jnp.dot(up_t[...], (av * uv).astype(BF16), preferred_element_type=F32)
            for b in range(2):
                rows[pl.ds(jj * 2 + b, RB, stride=16), :] = gd[:, b * 128 : b * 128 + 128]
            return carry
        for half in range(2):
            lax.fori_loop(0, 4, lambda jj, k: block(jj + 4 * half, k), 0, unroll=4)
            if half == 0:
                @pl.when(c > 0)
                def _():
                    step1(0, c - 1)
        def pack(big, carry):
            for idx in range(5):
                at = pl.ds(pl.multiple_of((big * 5 + idx) * 16, 16), 16)
                put(idx if idx < 4 else 14, big, c, rows[at, :].astype(BF16))
            return carry
        lax.fori_loop(0, 16, pack, 0, unroll=2)
        copy1(0, c).start()
        for at, what in ((2, gather_first), (3, lambda: gather_ring(1)), (5, lambda: gather_ring(2))):
            @pl.when(c == at)
            def _():
                what()
        return carry

    lax.fori_loop(0, PIECES, phase_a, 0)
    step1(0, PIECES - 1)
    def build(k):
        o = (z + 8 - k) % 8
        for u in range(3):
            copy_core(k, r, u).wait_recv()
            copy_core(k, mate, u).wait_recv()
        for u in range(3):
            off = EV * (8 * u + o) + 4
            for q in range(4):
                for t in range(9 if q < 3 else 6):
                    v = w[o, q, u, t * 16 : t * 16 + 16, :].astype(F32)
                    for half in range(2):
                        at = q * 144 + t * 16 + half * 8
                        if 2 * JIT <= at < 416:
                            wflat[pl.ds(off + at, 8), :] = v[half * 8 : half * 8 + 8]
                        else:
                            wflat[pl.ds(off + at, 8), :] += v[half * 8 : half * 8 + 8]
    gather_ring(3)
    build(0)
    for c in range(4):
        step2(0, c)
    gather_ring(4)
    for k in (1, 7):
        build(k)
    for c in range(4, PIECES):
        step2(0, c)
    hand_over(4)
    for k in (2, 6, 3, 5, 4):
        build(k)


    def phase_b(c, carry):
        def block(jj, carry):
            there = pl.ds(pl.multiple_of(c * 2048 + jj * 256, 256), 256)
            j = c * 16 + jj * 2
            wv = jnp.concatenate(
                [wflat[pl.ds(WPAD + j + b, RB, stride=NB), :] for b in range(2)], axis=1
            ).astype(BF16)
            dh = jnp.dot(up[...], wv, preferred_element_type=F32)
            gg = jnp.dot(tok_t[...], (dh * fac[:, there]).astype(BF16), preferred_element_type=F32)
            gu = jnp.dot(tok_t[...], (dh * act[:, there]).astype(BF16), preferred_element_type=F32)
            for m, v in enumerate((gg, gu)):
                for b in range(2):
                    rows[pl.ds(m * RB * 16 + jj * 2 + b, RB, stride=16), :] = v[:, b * 128 : b * 128 + 128]
            return carry
        for half in range(2):
            lax.fori_loop(0, 4, lambda jj, k: block(jj + 4 * half, k), 0, unroll=4)
            if half == 0:
                @pl.when(c > 0)
                def _():
                    step1(1, c - 1)
        def pack(big, carry):
            for n in range(4, 14):
                row = (n - 4) // 5 * RB + (n - 4) % 5
                at = pl.ds(pl.multiple_of((big * 5 + row) * 16, 16), 16)
                put(n, big, c, rows[at, :].astype(BF16))
            return carry
        lax.fori_loop(0, 16, pack, 0, unroll=2)
        copy1(1, c).start()
        step3(0, c)
        @pl.when(c > 2)
        def _():
            step2(1, c - 3)
        @pl.when(c > 3)
        def _():
            last_two(c - 4)
        return carry

    def last_two(c):
        step3(1, c)
        for d in range(1, 8):
            copy4(c, d).start()

    lax.fori_loop(0, PIECES, phase_b, 0)
    step1(1, PIECES - 1)

    for c in range(PIECES - 3, PIECES):
        step2(1, c)
        last_two(c - 1)
    last_two(PIECES - 1)

    def loop4(c, carry):
        for d in range(1, 8):
            copy4(c, d).wait_recv()
        v = a3[c, z // 4, z % 4]
        for d in range(7):
            v += c4[c, d]
        g[pl.ds(pl.multiple_of(c * 16, 16), 16), :] = v * (1.0 / 32768.0)
        return carry

    lax.fori_loop(0, PIECES, loop4, 0)

    n_own = member(z, core)
    real = n_own < 15
    own_m = matrix_of(n_own)
    i_own = (x * 4 + y) * 5 + index_of(n_own)
    row = own_m * RB + i_own
    ka, kb = z * 2 + core, x * 4 + y
    in_a = lambda d: (lambda k: device(x, y, k // 2, k % 2))((ka + d) % 16)
    in_b = lambda d: (lambda k: device(k // 4, k % 4, z, core))((kb + d) % 16)

    squares = g[...] * g[...]
    lane = lax.broadcasted_iota(jnp.int32, (1, 128), 1)
    last = jnp.where((lane == i_own) & real, jnp.sum(squares), 0.0) + wext[0:1, :]
    for k in range(16):
        sq[k, 0:7, :] = squares[7 * k : 7 * k + 7, :]
        sq[k, 7:8, :] = last

    def copy_a(d):
        return remote(sq.at[(ka + d) % 16], pa.at[d - 1], ssa.at[d - 1], rsa.at[d - 1], in_a(d))

    def copy_b(d):
        return remote(acc, pb.at[d - 1], ssb.at[d - 1], rsb.at[d - 1], in_b(d))

    def copy_c(d):
        return remote(pc.at[0, z], pc.at[0, z], ssc.at[d - 1], rsc.at[d - 1], along_z(d))

    def copy_d(d):
        return remote(pc.at[0, (z + 8 - d) % 8], pc.at[1, (z + 8 - d) % 8], ssd.at[d], rsd.at[d], other)

    for d in range(1, 16):
        copy_a(d).start()

    gv, qv = row // 15, row % 15

    def give(fn):
        for t in range(6):
            if t < 4:
                owner, k = 4 * gv + t, qv - BASES[t]
                ok = (k >= 0) & (k < COUNTS[t]) & real
                k = jnp.clip(k, 0, 5)
            elif t == 4:
                owner, k, ok = jnp.maximum(4 * gv - 1, 0), 5, (qv == 0) & (gv > 0) & real
            else:
                owner, k, ok = jnp.minimum(4 * gv + 4, 63), 0, (qv == 14) & (gv < 15) & real
            for half in range(2):
                fn(owner, k, ok, 2 * half + core, t * 2 + half)

    def send_row(owner, k, ok, rr, n):
        @pl.when(ok & ((owner != p) | (rr != r)))
        def _():
            remote(gb, gw.at[k], ssg.at[n], rsg.at[k], {"rep": rr, "dp": owner}).start()
        @pl.when(ok & (owner == p) & (rr == r))
        def _():
            gw[k] = gb[...]

    gb[...] = g[...].astype(BF16)
    give(send_row)

    a = p % 4
    base = 15 * (p // 4) + jnp.where(a == 0, -1, jnp.where(a == 1, 3, jnp.where(a == 2, 7, 10)))

    def window(arriving):
        for k in range(6):
            if k == 0:
                ok = p > 0
            elif k == 5:
                ok = (a == 0) | ((a == 3) & (p < 63))
            else:
                ok = p >= 0
            at = jnp.clip(base + k, 0, 239)
            m, idx = at // RB, at % 5
            from_core = jnp.where(m == 2, jnp.where(idx < 4, idx, 14), jnp.where(m == 0, 4 + idx, 9 + idx)) % 2
            hand = remote(gw.at[k], gw.at[k], ssf.at[k], rsf.at[k], other)
            if arriving:
                @pl.when(ok & (from_core == core) & ((base + k != row) | jnp.logical_not(real)))
                def _():
                    remote(gb, gw.at[k], ssg.at[k], rsg.at[k], other).wait_recv()
                @pl.when(ok & (from_core == core))
                def _():
                    hand.start()
                @pl.when(jnp.logical_not(ok))
                def _():
                    gw[k] = jnp.zeros((NB, 128), BF16)
            else:
                @pl.when(ok & (from_core != core))
                def _():
                    hand.wait_recv()
                @pl.when(ok & (from_core == core))
                def _():
                    hand.wait_send()

    def source(k):
        return matrix_of(member(k // 2, k % 2))

    v = sq[ka]
    for m in range(3):
        acc[m] = jnp.where(own_m == m, v, 0.0)
    for d in range(1, 16):
        copy_a(d).wait_recv()
        v = pa[d - 1]
        m_src = source((ka + 16 - d) % 16)
        for m in range(3):
            acc[m] += jnp.where(m_src == m, v, 0.0)
    for d in range(1, 16):
        copy_b(d).start()
    tot[...] = acc[...]
    for d in range(1, 16):
        copy_b(d).wait_recv()
        tot[...] += pb[d - 1]
    pc[0, z] = tot[...]
    for d in (4, 3, 5, 2, 6, 1, 7):
        copy_c(d).start()
    copy_d(0).start()
    extra[...] = tot[...]
    for d in (1, 7, 2, 6, 3, 5, 4):
        copy_c(d).wait_recv()
        copy_d(d).start()
    window(True)
    for d in range(8):
        copy_d(d).wait_recv()
    window(False)
    for k in range(8):
        for m in range(3):
            cols[m, 2 * k + core] = pc[0, k, m]
            cols[m, 2 * k + 1 - core] = pc[1, k, m]

    def wait_row(owner, k, ok, rr, n):
        @pl.when(ok & ((owner != p) | (rr != r)))
        def _():
            remote(gb, gw.at[k], ssg.at[n], rsg.at[k], {"rep": rr, "dp": owner}).wait_send()

    give(wait_row)
    for d in range(1, 16):
        copy_a(d).wait_send()
        copy_b(d).wait_send()
    for d in range(8):
        if d:
            copy_c(d).wait_send()
        copy_d(d).wait_send()

    @pl.when(p >= 40)
    def _():
        for d in range(1, 8):
            copy_spread(d).wait_send()

    for u in range(3):
        for s in range(1, 5):
            if s < 4 or u < 2:
                copy_up(s, u).wait_send()
            if s < 4 or u == 2:
                copy_down(s, u).wait_send()

    def drain_w(k, carry):
        for u in range(3):
            copy_y(k, u).wait_send()
            copy_core(k, r, u).wait_send()
            copy_core(k, mate, u).wait_send()
        return carry

    def drain(c, carry):
        for t in range(2):
            copy1(t, c).wait_send()
            for h in range(2):
                for d in (1, 2, 3):
                    copy2(t, c, h, d).wait_send()
                    copy3(t, c, h, d).wait_send()
        for d in range(1, 8):
            copy4(c, d).wait_send()
        return carry

    lax.fori_loop(0, 8, drain_w, 0)
    lax.fori_loop(0, PIECES, drain, 0)


def main(tokens, upstream, gate_pre, up_pre, quarter, wext):
    n = PIECES
    dma = lambda *shape: pltpu.SemaphoreType.DMA(shape)
    vm = pl.BlockSpec(memory_space=pltpu.VMEM)
    hbm = pl.BlockSpec(memory_space=pl.ANY)
    both = lambda *shape: [pltpu.VMEM(shape[:-1] + (k * shape[-1], 16, 128), BF16) for k in (1, 3)]
    return pl.pallas_call(
        main_kernel,
        in_specs=[vm, vm, hbm, hbm, vm, vm],
        out_specs=[vm, vm, vm],
        out_shape=[
            jax.ShapeDtypeStruct((6, NB, 128), BF16),
            jax.ShapeDtypeStruct((3, 16, 8, 128), F32),
            jax.ShapeDtypeStruct((3, 8, 128), F32),
        ],
        scratch_shapes=[
            pltpu.VMEM((n, 128, 2048), BF16),
            pltpu.VMEM((n, 128, 2048), BF16),
            pltpu.VMEM((128, 14336), F32),
            pltpu.VMEM((128, 14336), F32),
            pltpu.VMEM((8, 4, 3, 144, 128), BF16),
            pltpu.VMEM((WROWS, 128), F32),
            pltpu.VMEM((2 * RB * 16, 128), F32),
            *both(n, 2, 2, 4, 4),
            *both(n, 2, 4, 4),
            *both(n, 2, 4, 4),
            *both(n, 2, 3, 4),
            *both(n, 2, 4, 1),
            pltpu.VMEM((4, 1, 16, 128), F32),
            pltpu.VMEM((4, 3, 16, 128), F32),
            *both(n, 2, 3, 1),
            pltpu.VMEM((n, 2, 4, 16, 128), F32),
            pltpu.VMEM((n, 7, 16, 128), F32),
            pltpu.VMEM((128, RB), BF16),
            pltpu.VMEM((NB, 128), F32),
            pltpu.VMEM((NB, 128), BF16),
            pltpu.VMEM((16, 8, 128), F32),
            pltpu.VMEM((15, 8, 128), F32),
            pltpu.VMEM((3, 8, 128), F32),
            pltpu.VMEM((15, 3, 8, 128), F32),
            pltpu.VMEM((3, 8, 128), F32),
            pltpu.VMEM((2, 8, 3, 8, 128), F32),
            dma(n), dma(n),
            dma(7), dma(3), dma(12), dma(12), dma(12), dma(12), dma(24), dma(24), dma(48), dma(48),
            dma(2 * n), dma(2 * n), dma(2 * n, 6), dma(2 * n, 6), dma(2 * n, 6), dma(2 * n, 6), dma(n, 7), dma(n, 7),
            dma(15), dma(15), dma(15), dma(15), dma(7), dma(7), dma(8), dma(8), dma(12), dma(6), dma(6), dma(6),
        ],
        compiler_params=pltpu.CompilerParams(
            vmem_limit_bytes=VMEM_LIMIT, collective_id=0, has_side_effects=True
        ),
        name="main",
    )(tokens.T, upstream.T, gate_pre, up_pre, quarter, wext)


def update_kernel(lengths, gw, cols, extra, params, row_state, col_state, out_p, out_d, out_r, out_c, moved, scaled, held):
    p = lax.axis_index("dp")
    start, length = span(lengths)
    a = p % 4
    first = 15 * (p // 4) + jnp.where(a == 0, -1, jnp.where(a == 1, 3, jnp.where(a == 2, 7, 10)))
    shift = start - NB * first
    for m in range(3):
        for k in range(16):
            part = pl.ds(m * NB + 7 * k, 7)
            out_c[part, :] = BETA * col_state[part, :] + (1.0 - BETA) * (cols[m, k, 0:7, :] * (1.0 / RB) + TINY)
    lane = lax.broadcasted_iota(jnp.int32, (1, 128), 1)
    sums_row = extra[:, 7, :]
    live = lax.broadcasted_iota(jnp.int32, (3, 128), 1) < RB
    for m in range(3):
        held[m : m + 1, 0:RB] = row_state[:, m * RB : m * RB + RB]
    rows = jnp.where(live, BETA * held[...] + (1.0 - BETA) * (sums_row * (1.0 / 14336.0) + TINY), 0.0)
    for m in range(3):
        out_r[:, m * RB : m * RB + RB] = rows[m : m + 1, 0:RB]
    means = jnp.sum(rows, axis=1, keepdims=True) * (1.0 / RB)
    weight = jnp.sum(sums_row, axis=0, keepdims=True)
    for k in range(6):
        row = jnp.clip(first + k, 0, 239)
        m = row // RB
        i = row % RB
        pick = lambda v: jnp.where(m == 0, v[0:1], jnp.where(m == 1, v[1:2], v[2:3]))
        value = jnp.sum(jnp.where(lane == i, pick(rows), 0.0), axis=1, keepdims=True)
        sq = jnp.sum(jnp.where(lane == 120 + m, weight, 0.0), axis=1, keepdims=True)
        scale = RHO * jnp.sqrt(sq * (1.0 / (RB * 14336.0)))
        factor = value / pick(means)
        v = gw[k].astype(F32) * lax.rsqrt(factor * out_c[pl.ds(pl.multiple_of(m * NB, 8), NB), :])
        moved[pl.ds(k * NB, NB), :] = v
        scaled[pl.ds(k * NB, NB), :] = scale * v
    def tile(t, carry):
        o = pl.multiple_of(t * 16, 16)
        at = pl.ds(shift + o, 16)
        keep = o + lax.broadcasted_iota(jnp.int32, (16, 128), 0) < length
        out_d[pl.ds(o, 16), :] = jnp.where(keep, moved[at, :], 0.0).astype(BF16)
        new = params[pl.ds(o, 16), :].astype(F32) - scaled[at, :]
        out_p[pl.ds(o, 16), :] = jnp.where(keep, new, 0.0).astype(BF16)
        return carry
    lax.fori_loop(0, 34, tile, 0)


def update(lengths, gw, cols, extra, params, row_state, col_state):
    vm = pl.BlockSpec(memory_space=pltpu.VMEM)
    return pl.pallas_call(
        update_kernel,
        in_specs=[pl.BlockSpec(memory_space=pltpu.SMEM)] + [vm] * 6,
        out_specs=[vm] * 4,
        out_shape=[
            jax.ShapeDtypeStruct((544, 128), BF16),
            jax.ShapeDtypeStruct((544, 128), BF16),
            jax.ShapeDtypeStruct((1, 240), F32),
            jax.ShapeDtypeStruct((336, 128), F32),
        ],
        scratch_shapes=[pltpu.VMEM((800, 128), F32), pltpu.VMEM((800, 128), F32), pltpu.VMEM((3, 128), F32)],
        compiler_params=pltpu.CompilerParams(vmem_limit_bytes=VMEM_LIMIT),
        name="update",
    )(lengths, gw, cols, extra, params, row_state, col_state)


def body(tokens, upstream, gate_pre, up_pre, param_shards, shard_rows, row_state, col_state):
    quarter, wext = prep(shard_rows, param_shards)
    gw, cols, extra = main(tokens, upstream, gate_pre, up_pre, quarter, wext)
    new_params, direction, rows, new_cols = update(
        shard_rows, gw, cols, extra, param_shards, row_state.reshape(1, 240), col_state.reshape(336, 128)
    )
    return (new_params, direction, rows.reshape(-1), new_cols.reshape(-1))


def solution(mesh):
    in_specs = (
        P(("rep", "dp"), None),
        P(("rep", "dp"), None),
        P(("rep", "dp"), None),
        P(("rep", "dp"), None),
        P("dp", None),
        P(),
        P(),
        P(),
    )
    out_specs = (P("dp", None), P("dp", None), P(), P())
    return jax.shard_map(body, mesh=mesh, in_specs=in_specs, out_specs=out_specs, check_vma=False)
```

```python
import functools

import jax
import jax.numpy as jnp
from jax import lax
from jax.experimental import pallas as pl
from jax.experimental.pallas import tpu as pltpu
from jax.sharding import PartitionSpec as P

BETA = 0.8
RHO = 0.2
TINY = 1e-30
RB = 80
NB = 112
EV = 420
JIT = 52
PIECES = 7
WPAD = 1176
WROWS = 10200
BASES = (-1, 3, 7, 10)
COUNTS = (6, 5, 5, 6)
F32 = jnp.float32
BF16 = jnp.bfloat16
VMEM_LIMIT = 60 * 1024 * 1024


def coords():
    r = lax.axis_index("rep")
    p = lax.axis_index("dp")
    x = p // 16
    y = (p // 8 % 2) * 2 + r // 2
    return x, y, p % 8, r % 2


def device(x, y, z, core):
    return {"rep": (y % 2) * 2 + core, "dp": (x * 2 + y // 2) * 8 + z}


def hello(targets):
    barrier = pltpu.get_barrier_semaphore()
    for target in targets:
        pl.semaphore_signal(barrier, inc=1, device_id=target, device_id_type=pl.DeviceIdType.MESH)


def remote(src, dst, send, recv, target):
    return pltpu.make_async_remote_copy(
        src_ref=src, dst_ref=dst, send_sem=send, recv_sem=recv,
        device_id=target, device_id_type=pl.DeviceIdType.MESH,
    )


def span(lengths):
    p = lax.axis_index("dp")
    add = lambda k, total: total + jnp.where(k < p, lengths[k], 0)
    start = lax.fori_loop(0, 64, add, jnp.int32(0), unroll=8)
    return start, lengths[p]


def prep_kernel(lengths, params, quarter, wext, shifted):
    p, r = lax.axis_index("dp"), lax.axis_index("rep")
    start, length = span(lengths)
    row = lax.broadcasted_iota(jnp.int32, (544, 128), 0)
    v = jnp.where(row < length, params[...].astype(F32), 0.0)
    shifted[0 : 2 * JIT, :] = jnp.zeros((2 * JIT, 128), F32)
    shifted[2 * JIT : 2 * JIT + 544, :] = v
    shifted[2 * JIT + 544 :, :] = jnp.zeros((72, 128), F32)
    at = jnp.clip(2 * JIT - (start - (EV * p - JIT)) + 144 * r, 0, 576)
    quarter[...] = shifted[pl.ds(at, 144), :].astype(BF16)
    v = v * v
    flat = row + start
    lane = lax.broadcasted_iota(jnp.int32, (8, 128), 1)
    total = jnp.zeros((8, 128), F32)
    for m in range(3):
        inside = (flat >= m * 8960) & (flat < m * 8960 + 8960)
        total += jnp.where(lane == 120 + m, 0.25 * jnp.sum(jnp.where(inside, v, 0.0)), 0.0)
    wext[...] = total


def prep(shard_rows, params):
    vm = pl.BlockSpec(memory_space=pltpu.VMEM)
    return pl.pallas_call(
        prep_kernel,
        in_specs=[pl.BlockSpec(memory_space=pltpu.SMEM), vm],
        out_specs=[vm, vm],
        out_shape=[jax.ShapeDtypeStruct((144, 128), BF16), jax.ShapeDtypeStruct((8, 128), F32)],
        scratch_shapes=[pltpu.VMEM((720, 128), F32)],
        compiler_params=pltpu.CompilerParams(vmem_limit_bytes=VMEM_LIMIT),
        name="prep",
    )(shard_rows, params)


def matrix_of(n):
    return jnp.where(n < 4, 2, jnp.where(n < 9, 0, jnp.where(n < 14, 1, 2)))


def index_of(n):
    return jnp.where(n < 4, n, jnp.where(n < 9, n - 4, jnp.where(n < 14, n - 9, 4)))


def member(z, core):
    return z % 4 * 4 + z // 4 * 2 + core


def main_kernel(
    tok_t, up_t, gate_hbm, upp_hbm, quarter, wext, gw, cols, extra,
    gate, upp, act, fac, w, wflat, rows, fa, fb, c1a, c1b, a1a, a1b, c2a, c2b, a2a, a2b, own2a, own2b,
    c3a, c3b, a3, c4, up, g, gb, sq, pa, acc, pb, tot, pc,
    sg, su, w1, v1, wp, vp, wm, vm, wy, vy, wc, vc,
    s1, r1, s2, r2, s3, r3, s4, r4, ssa, rsa, ssb, rsb, ssc, rsc, ssd, rsd, ssg, rsg, ssf, rsf,
):
    x, y, z, core = coords()
    r, p = lax.axis_index("rep"), lax.axis_index("dp")
    plane = p // 8
    other = device(x, y, z, 1 - core)
    along_x = lambda d: device((x + d) % 4, y, z, core)
    along_y = lambda d: device(x, (y + d) % 4, z, core)
    along_z = lambda d: device(x, y, (z + d) % 8, core)

    def load(c):
        part = pl.ds(pl.multiple_of(c * 2048, 2048), 2048)
        return (
            pltpu.make_async_copy(gate_hbm.at[:, part], gate.at[c], sg.at[c]),
            pltpu.make_async_copy(upp_hbm.at[:, part], upp.at[c], su.at[c]),
        )

    def begin(c, carry):
        for copy in load(c):
            copy.start()
        return carry

    lax.fori_loop(0, PIECES, begin, 0)
    hello(
        [other]
        + [along_x(d) for d in (1, 2, 3)]
        + [along_y(d) for d in (1, 2, 3)]
        + [along_z(d) for d in range(1, 8)]
        + [device((x + d) % 4, (y + 2) % 4, z, core) for d in (1, 2, 3)]
    )
    pl.semaphore_wait(pltpu.get_barrier_semaphore(), 17)

    spread = lambda d: {"rep": r, "dp": (plane + d) % 8 * 8 + z}
    mate = (1 - r // 2) * 2 + core

    def copy_spread(d):
        return remote(quarter, w.at[z, r, jnp.maximum(plane - 5, 0)], w1.at[d - 1], v1.at[jnp.maximum(plane - 5, 0)], spread(d))

    def copy_up(s, u):
        block = w.at[(z + 9 - s) % 8, r, u]
        n = (s - 1) * 3 + u
        return remote(block, block, wp.at[n], vp.at[n], along_z(1))

    def copy_down(s, u):
        block = w.at[(z + s - 1) % 8, r, u]
        n = (s - 1) * 3 + u
        return remote(block, block, wm.at[n], vm.at[n], along_z(7))

    def copy_y(k, u):
        block = w.at[(z + 8 - k) % 8, r, u]
        to = jnp.where((k == 0) | (k > 4), 3, 1)
        return remote(block, block, wy.at[k * 3 + u], vy.at[k * 3 + u], along_y(to))

    def copy_core(k, q, u):
        block = w.at[(z + 8 - k) % 8, q, u]
        n = (jnp.where(q == r, 0, 8) + k) * 3 + u
        return remote(block, block, wc.at[n], vc.at[n], other)

    @pl.when(p >= 40)
    def _():
        for d in range(1, 8):
            copy_spread(d).start()
        w[z, r, jnp.maximum(plane - 5, 0)] = quarter[...]

    def gather_first():
        for u in range(3):
            @pl.when(plane != 5 + u)
            def _():
                remote(quarter, w.at[z, r, u], w1.at[0], v1.at[u], spread(1)).wait_recv()
            copy_up(1, u).start()
            copy_down(1, u).start()
        for u in range(3):
            copy_y(0, u).start()
        for u in range(3):
            copy_core(0, r, u).start()

    def gather_ring(s):
        for u in range(3):
            for copy, last in ((copy_up, u < 2), (copy_down, u == 2)):
                if s < 4 or last:
                    copy(s, u).wait_recv()
                if s < 3 or (s == 3 and last):
                    copy(s + 1, u).start()
        for u in range(3):
            copy_y(s, u).start()
            if s < 4:
                copy_y(8 - s, u).start()
        for u in range(3):
            copy_core(s, r, u).start()
            if s < 4:
                copy_core(8 - s, r, u).start()
        hand_over(s - 1)
        if s > 1:
            hand_over(9 - s)

    def hand_over(k):
        for u in range(3):
            copy_y(k, u).wait_recv()
            copy_core(k, mate, u).start()

    f, c1, a1, c2 = (fa, fb), (c1a, c1b), (a1a, a1b), (c2a, c2b)
    a2, own2, c3 = (a2a, a2b), (own2a, own2b), (c3a, c3b)
    first, second = (x, y), (y, x)
    axis_of = (along_x, along_y)

    def copy1(t, c):
        k = t * PIECES + c
        return remote(f[t].at[c, 1 - core], c1[t].at[c], s1.at[k], r1.at[k], other)

    def copy2(t, c, h, d):
        k, n = t * PIECES + c, h * 3 + d - 1
        return remote(a1[t].at[c, h, (first[h] + d) % 4], c2[t].at[c, h, d - 1], s2.at[k, n], r2.at[k, n], axis_of[h](d))

    def copy3(t, c, h, d):
        k, n = t * PIECES + c, h * 3 + d - 1
        return remote(a2[t].at[c, h, (second[h] + d) % 4], c3[t].at[c, h, d - 1], s3.at[k, n], r3.at[k, n], axis_of[1 - h](d))

    def copy4(c, d):
        to = (z + d) % 8
        return remote(a3.at[c, to // 4, to % 4], c4.at[c, d - 1], s4.at[c, d - 1], r4.at[c, d - 1], along_z(d))

    def step1(t, c):
        copy1(t, c).wait_recv()
        for h in range(2):
            def add(i, carry):
                a1[t][c, h, i] = (f[t][c, core, h, i].astype(F32) + c1[t][c, h, i].astype(F32)).astype(BF16)
                return carry
            lax.fori_loop(0, 4, add, 0)
            for d in (1, 2, 3):
                copy2(t, c, h, d).start()

    def step2(t, c):
        nz = (1, 3)[t]
        for h in range(2):
            for d in (1, 2, 3):
                copy2(t, c, h, d).wait_recv()
            def add(i, carry):
                part = pl.ds(i * nz, nz)
                v = f[t][c, core, h, first[h], part].astype(F32) + c1[t][c, h, first[h], part].astype(F32)
                for d in range(3):
                    v += c2[t][c, h, d, part].astype(F32)
                a2[t][c, h, i] = v.astype(BF16)
                own2[t][i] = v
                return carry
            lax.fori_loop(0, 4, add, 0)
            a3[c, h, pl.ds(t, nz)] = own2[t][second[h]]
            for d in (1, 2, 3):
                copy3(t, c, h, d).start()

    def step3(t, c):
        nz = (1, 3)[t]
        for h in range(2):
            for d in (1, 2, 3):
                copy3(t, c, h, d).wait_recv()
            v = a3[c, h, pl.ds(t, nz)]
            for d in range(3):
                v += c3[t][c, h, d].astype(F32)
            a3[c, h, pl.ds(t, nz)] = v

    def put(n, big, c, v):
        core_of, h, zz = n % 2, n // 2 % 2, n // 4
        one, two = (big // 4, big % 4) if h == 0 else (big % 4, big // 4)
        if zz == 0:
            fa[c, core_of, h, one, two] = v
        else:
            fb[c, core_of, h, one, two * 3 + zz - 1] = v

    wflat[...] = jnp.zeros_like(wflat)
    up[...] = up_t[...].astype(F32).T.astype(BF16)
    def clear(c, carry):
        def one(i, carry):
            for j in range(4):
                fb[c, 1, 1, i, j * 3 + 2] = jnp.zeros((16, 128), BF16)
            return carry
        return lax.fori_loop(0, 4, one, carry)
    lax.fori_loop(0, PIECES, clear, 0)

    def phase_a(c, carry):
        for copy in load(c):
            copy.wait()
        def block(jj, carry):
            here = pl.ds(pl.multiple_of(jj * 256, 256), 256)
            there = pl.ds(pl.multiple_of(c * 2048 + jj * 256, 256), 256)
            gv = gate[c, :, here].astype(F32)
            uv = upp[c, :, here].astype(F32)
            s = 0.5 * jnp.tanh(0.5 * gv) + 0.5
            av = gv * s
            act[:, there] = av
            fac[:, there] = uv * s * (1.0 + gv * (1.0 - s))
            gd = jnp.dot(up_t[...], (av * uv).astype(BF16), preferred_element_type=F32)
            for b in range(2):
                rows[pl.ds(jj * 2 + b, RB, stride=16), :] = gd[:, b * 128 : b * 128 + 128]
            return carry
        for half in range(2):
            lax.fori_loop(0, 4, lambda jj, k: block(jj + 4 * half, k), 0, unroll=4)
            if half == 0:
                @pl.when(c > 0)
                def _():
                    step1(0, c - 1)
        def pack(big, carry):
            for idx in range(5):
                at = pl.ds(pl.multiple_of((big * 5 + idx) * 16, 16), 16)
                put(idx if idx < 4 else 14, big, c, rows[at, :].astype(BF16))
            return carry
        lax.fori_loop(0, 16, pack, 0, unroll=2)
        copy1(0, c).start()
        for at, what in ((2, gather_first), (3, lambda: gather_ring(1)), (5, lambda: gather_ring(2))):
            @pl.when(c == at)
            def _():
                what()
        return carry

    lax.fori_loop(0, PIECES, phase_a, 0)
    step1(0, PIECES - 1)
    def build(k):
        o = (z + 8 - k) % 8
        for u in range(3):
            copy_core(k, r, u).wait_recv()
            copy_core(k, mate, u).wait_recv()
        for u in range(3):
            off = EV * (8 * u + o) + 4
            for q in range(4):
                for t in range(9 if q < 3 else 6):
                    v = w[o, q, u, t * 16 : t * 16 + 16, :].astype(F32)
                    for half in range(2):
                        at = q * 144 + t * 16 + half * 8
                        if 2 * JIT <= at < 416:
                            wflat[pl.ds(off + at, 8), :] = v[half * 8 : half * 8 + 8]
                        else:
                            wflat[pl.ds(off + at, 8), :] += v[half * 8 : half * 8 + 8]
    gather_ring(3)
    build(0)
    for c in range(4):
        step2(0, c)
    gather_ring(4)
    for k in (1, 7):
        build(k)
    for c in range(4, PIECES):
        step2(0, c)
    hand_over(4)
    for k in (2, 6, 3, 5, 4):
        build(k)


    def phase_b(c, carry):
        def block(jj, carry):
            there = pl.ds(pl.multiple_of(c * 2048 + jj * 256, 256), 256)
            j = c * 16 + jj * 2
            wv = jnp.concatenate(
                [wflat[pl.ds(WPAD + j + b, RB, stride=NB), :] for b in range(2)], axis=1
            ).astype(BF16)
            dh = jnp.dot(up[...], wv, preferred_element_type=F32)
            gg = jnp.dot(tok_t[...], (dh * fac[:, there]).astype(BF16), preferred_element_type=F32)
            gu = jnp.dot(tok_t[...], (dh * act[:, there]).astype(BF16), preferred_element_type=F32)
            for m, v in enumerate((gg, gu)):
                for b in range(2):
                    rows[pl.ds(m * RB * 16 + jj * 2 + b, RB, stride=16), :] = v[:, b * 128 : b * 128 + 128]
            return carry
        for half in range(2):
            lax.fori_loop(0, 4, lambda jj, k: block(jj + 4 * half, k), 0, unroll=4)
            if half == 0:
                @pl.when(c > 0)
                def _():
                    step1(1, c - 1)
        def pack(big, carry):
            for n in range(4, 14):
                row = (n - 4) // 5 * RB + (n - 4) % 5
                at = pl.ds(pl.multiple_of((big * 5 + row) * 16, 16), 16)
                put(n, big, c, rows[at, :].astype(BF16))
            return carry
        lax.fori_loop(0, 16, pack, 0, unroll=2)
        copy1(1, c).start()
        step3(0, c)
        @pl.when(c > 2)
        def _():
            step2(1, c - 3)
        @pl.when(c > 3)
        def _():
            last_two(c - 4)
        return carry

    def last_two(c):
        step3(1, c)
        for d in range(1, 8):
            copy4(c, d).start()

    lax.fori_loop(0, PIECES, phase_b, 0)
    step1(1, PIECES - 1)

    for c in range(PIECES - 3, PIECES):
        step2(1, c)
        last_two(c - 1)
    last_two(PIECES - 1)

    def loop4(c, carry):
        for d in range(1, 8):
            copy4(c, d).wait_recv()
        v = a3[c, z // 4, z % 4]
        for d in range(7):
            v += c4[c, d]
        g[pl.ds(pl.multiple_of(c * 16, 16), 16), :] = v * (1.0 / 32768.0)
        return carry

    lax.fori_loop(0, PIECES, loop4, 0)

    n_own = member(z, core)
    real = n_own < 15
    own_m = matrix_of(n_own)
    i_own = (x * 4 + y) * 5 + index_of(n_own)
    row = own_m * RB + i_own
    ka, kb = z * 2 + core, x * 4 + y
    in_a = lambda d: (lambda k: device(x, y, k // 2, k % 2))((ka + d) % 16)
    in_b = lambda d: (lambda k: device(k // 4, k % 4, z, core))((kb + d) % 16)

    squares = g[...] * g[...]
    lane = lax.broadcasted_iota(jnp.int32, (1, 128), 1)
    last = jnp.where((lane == i_own) & real, jnp.sum(squares), 0.0) + wext[0:1, :]
    for k in range(16):
        sq[k, 0:7, :] = squares[7 * k : 7 * k + 7, :]
        sq[k, 7:8, :] = last

    def copy_a(d):
        return remote(sq.at[(ka + d) % 16], pa.at[d - 1], ssa.at[d - 1], rsa.at[d - 1], in_a(d))

    def copy_b(d):
        return remote(acc, pb.at[d - 1], ssb.at[d - 1], rsb.at[d - 1], in_b(d))

    def copy_c(d):
        return remote(pc.at[0, z], pc.at[0, z], ssc.at[d - 1], rsc.at[d - 1], along_z(d))

    def copy_d(d):
        return remote(pc.at[0, (z + 8 - d) % 8], pc.at[1, (z + 8 - d) % 8], ssd.at[d], rsd.at[d], other)

    for d in range(1, 16):
        copy_a(d).start()

    gv, qv = row // 15, row % 15

    def give(fn):
        for t in range(6):
            if t < 4:
                owner, k = 4 * gv + t, qv - BASES[t]
                ok = (k >= 0) & (k < COUNTS[t]) & real
                k = jnp.clip(k, 0, 5)
            elif t == 4:
                owner, k, ok = jnp.maximum(4 * gv - 1, 0), 5, (qv == 0) & (gv > 0) & real
            else:
                owner, k, ok = jnp.minimum(4 * gv + 4, 63), 0, (qv == 14) & (gv < 15) & real
            for half in range(2):
                fn(owner, k, ok, 2 * half + core, t * 2 + half)

    def send_row(owner, k, ok, rr, n):
        @pl.when(ok & ((owner != p) | (rr != r)))
        def _():
            remote(gb, gw.at[k], ssg.at[n], rsg.at[k], {"rep": rr, "dp": owner}).start()
        @pl.when(ok & (owner == p) & (rr == r))
        def _():
            gw[k] = gb[...]

    gb[...] = g[...].astype(BF16)
    give(send_row)

    @pl.when(p >= 40)
    def _():
        for d in range(1, 8):
            copy_spread(d).wait_send()

    for u in range(3):
        for s in range(1, 5):
            if s < 4 or u < 2:
                copy_up(s, u).wait_send()
            if s < 4 or u == 2:
                copy_down(s, u).wait_send()

    def drain_w(k, carry):
        for u in range(3):
            copy_y(k, u).wait_send()
            copy_core(k, r, u).wait_send()
            copy_core(k, mate, u).wait_send()
        return carry

    def drain(c, carry):
        for t in range(2):
            copy1(t, c).wait_send()
            for h in range(2):
                for d in (1, 2, 3):
                    copy2(t, c, h, d).wait_send()
                    copy3(t, c, h, d).wait_send()
        for d in range(1, 8):
            copy4(c, d).wait_send()
        return carry

    lax.fori_loop(0, 8, drain_w, 0)
    lax.fori_loop(0, PIECES, drain, 0)

    a = p % 4
    base = 15 * (p // 4) + jnp.where(a == 0, -1, jnp.where(a == 1, 3, jnp.where(a == 2, 7, 10)))

    def window(arriving):
        for k in range(6):
            if k == 0:
                ok = p > 0
            elif k == 5:
                ok = (a == 0) | ((a == 3) & (p < 63))
            else:
                ok = p >= 0
            at = jnp.clip(base + k, 0, 239)
            m, idx = at // RB, at % 5
            from_core = jnp.where(m == 2, jnp.where(idx < 4, idx, 14), jnp.where(m == 0, 4 + idx, 9 + idx)) % 2
            hand = remote(gw.at[k], gw.at[k], ssf.at[k], rsf.at[k], other)
            if arriving:
                @pl.when(ok & (from_core == core) & ((base + k != row) | jnp.logical_not(real)))
                def _():
                    remote(gb, gw.at[k], ssg.at[k], rsg.at[k], other).wait_recv()
                @pl.when(ok & (from_core == core))
                def _():
                    hand.start()
                @pl.when(jnp.logical_not(ok))
                def _():
                    gw[k] = jnp.zeros((NB, 128), BF16)
            else:
                @pl.when(ok & (from_core != core))
                def _():
                    hand.wait_recv()
                @pl.when(ok & (from_core == core))
                def _():
                    hand.wait_send()

    def source(k):
        return matrix_of(member(k // 2, k % 2))

    v = sq[ka]
    for m in range(3):
        acc[m] = jnp.where(own_m == m, v, 0.0)
    for d in range(1, 16):
        copy_a(d).wait_recv()
        v = pa[d - 1]
        m_src = source((ka + 16 - d) % 16)
        for m in range(3):
            acc[m] += jnp.where(m_src == m, v, 0.0)
    for d in range(1, 16):
        copy_b(d).start()
    for d in range(1, 16):
        copy_a(d).wait_send()
    tot[...] = acc[...]
    for d in range(1, 16):
        copy_b(d).wait_recv()
        tot[...] += pb[d - 1]
    pc[0, z] = tot[...]
    for d in (4, 3, 5, 2, 6, 1, 7):
        copy_c(d).start()
    copy_d(0).start()
    extra[...] = tot[...]

    def wait_row(owner, k, ok, rr, n):
        @pl.when(ok & ((owner != p) | (rr != r)))
        def _():
            remote(gb, gw.at[k], ssg.at[n], rsg.at[k], {"rep": rr, "dp": owner}).wait_send()

    give(wait_row)
    for d in range(1, 16):
        copy_b(d).wait_send()
    for d in (1, 7, 2, 6, 3, 5, 4):
        copy_c(d).wait_recv()
        copy_d(d).start()
    window(True)
    for d in range(8):
        copy_d(d).wait_recv()
    window(False)
    for k in range(8):
        for m in range(3):
            cols[m, 2 * k + core] = pc[0, k, m]
            cols[m, 2 * k + 1 - core] = pc[1, k, m]
    for d in range(8):
        if d:
            copy_c(d).wait_send()
        copy_d(d).wait_send()


def main(tokens, upstream, gate_pre, up_pre, quarter, wext):
    n = PIECES
    dma = lambda *shape: pltpu.SemaphoreType.DMA(shape)
    vm = pl.BlockSpec(memory_space=pltpu.VMEM)
    hbm = pl.BlockSpec(memory_space=pl.ANY)
    both = lambda *shape: [pltpu.VMEM(shape[:-1] + (k * shape[-1], 16, 128), BF16) for k in (1, 3)]
    return pl.pallas_call(
        main_kernel,
        in_specs=[vm, vm, hbm, hbm, vm, vm],
        out_specs=[vm, vm, vm],
        out_shape=[
            jax.ShapeDtypeStruct((6, NB, 128), BF16),
            jax.ShapeDtypeStruct((3, 16, 8, 128), F32),
            jax.ShapeDtypeStruct((3, 8, 128), F32),
        ],
        scratch_shapes=[
            pltpu.VMEM((n, 128, 2048), BF16),
            pltpu.VMEM((n, 128, 2048), BF16),
            pltpu.VMEM((128, 14336), F32),
            pltpu.VMEM((128, 14336), F32),
            pltpu.VMEM((8, 4, 3, 144, 128), BF16),
            pltpu.VMEM((WROWS, 128), F32),
            pltpu.VMEM((2 * RB * 16, 128), F32),
            *both(n, 2, 2, 4, 4),
            *both(n, 2, 4, 4),
            *both(n, 2, 4, 4),
            *both(n, 2, 3, 4),
            *both(n, 2, 4, 1),
            pltpu.VMEM((4, 1, 16, 128), F32),
            pltpu.VMEM((4, 3, 16, 128), F32),
            *both(n, 2, 3, 1),
            pltpu.VMEM((n, 2, 4, 16, 128), F32),
            pltpu.VMEM((n, 7, 16, 128), F32),
            pltpu.VMEM((128, RB), BF16),
            pltpu.VMEM((NB, 128), F32),
            pltpu.VMEM((NB, 128), BF16),
            pltpu.VMEM((16, 8, 128), F32),
            pltpu.VMEM((15, 8, 128), F32),
            pltpu.VMEM((3, 8, 128), F32),
            pltpu.VMEM((15, 3, 8, 128), F32),
            pltpu.VMEM((3, 8, 128), F32),
            pltpu.VMEM((2, 8, 3, 8, 128), F32),
            dma(n), dma(n),
            dma(7), dma(3), dma(12), dma(12), dma(12), dma(12), dma(24), dma(24), dma(48), dma(48),
            dma(2 * n), dma(2 * n), dma(2 * n, 6), dma(2 * n, 6), dma(2 * n, 6), dma(2 * n, 6), dma(n, 7), dma(n, 7),
            dma(15), dma(15), dma(15), dma(15), dma(7), dma(7), dma(8), dma(8), dma(12), dma(6), dma(6), dma(6),
        ],
        compiler_params=pltpu.CompilerParams(
            vmem_limit_bytes=VMEM_LIMIT, collective_id=0, has_side_effects=True
        ),
        name="main",
    )(tokens.T, upstream.T, gate_pre, up_pre, quarter, wext)


def update_kernel(lengths, gw, cols, extra, params, row_state, col_state, out_p, out_d, out_r, out_c, moved, scaled, held):
    p = lax.axis_index("dp")
    start, length = span(lengths)
    a = p % 4
    first = 15 * (p // 4) + jnp.where(a == 0, -1, jnp.where(a == 1, 3, jnp.where(a == 2, 7, 10)))
    shift = start - NB * first
    for m in range(3):
        for k in range(16):
            part = pl.ds(m * NB + 7 * k, 7)
            out_c[part, :] = BETA * col_state[part, :] + (1.0 - BETA) * (cols[m, k, 0:7, :] * (1.0 / RB) + TINY)
    lane = lax.broadcasted_iota(jnp.int32, (1, 128), 1)
    sums_row = extra[:, 7, :]
    live = lax.broadcasted_iota(jnp.int32, (3, 128), 1) < RB
    for m in range(3):
        held[m : m + 1, 0:RB] = row_state[:, m * RB : m * RB + RB]
    rows = jnp.where(live, BETA * held[...] + (1.0 - BETA) * (sums_row * (1.0 / 14336.0) + TINY), 0.0)
    for m in range(3):
        out_r[:, m * RB : m * RB + RB] = rows[m : m + 1, 0:RB]
    means = jnp.sum(rows, axis=1, keepdims=True) * (1.0 / RB)
    weight = jnp.sum(sums_row, axis=0, keepdims=True)
    for k in range(6):
        row = jnp.clip(first + k, 0, 239)
        m = row // RB
        i = row % RB
        pick = lambda v: jnp.where(m == 0, v[0:1], jnp.where(m == 1, v[1:2], v[2:3]))
        value = jnp.sum(jnp.where(lane == i, pick(rows), 0.0), axis=1, keepdims=True)
        sq = jnp.sum(jnp.where(lane == 120 + m, weight, 0.0), axis=1, keepdims=True)
        scale = RHO * jnp.sqrt(sq * (1.0 / (RB * 14336.0)))
        factor = value / pick(means)
        v = gw[k].astype(F32) * lax.rsqrt(factor * out_c[pl.ds(pl.multiple_of(m * NB, 8), NB), :])
        moved[pl.ds(k * NB, NB), :] = v
        scaled[pl.ds(k * NB, NB), :] = scale * v
    def tile(t, carry):
        o = pl.multiple_of(t * 16, 16)
        at = pl.ds(shift + o, 16)
        keep = o + lax.broadcasted_iota(jnp.int32, (16, 128), 0) < length
        out_d[pl.ds(o, 16), :] = jnp.where(keep, moved[at, :], 0.0).astype(BF16)
        new = params[pl.ds(o, 16), :].astype(F32) - scaled[at, :]
        out_p[pl.ds(o, 16), :] = jnp.where(keep, new, 0.0).astype(BF16)
        return carry
    lax.fori_loop(0, 34, tile, 0)


def update(lengths, gw, cols, extra, params, row_state, col_state):
    vm = pl.BlockSpec(memory_space=pltpu.VMEM)
    return pl.pallas_call(
        update_kernel,
        in_specs=[pl.BlockSpec(memory_space=pltpu.SMEM)] + [vm] * 6,
        out_specs=[vm] * 4,
        out_shape=[
            jax.ShapeDtypeStruct((544, 128), BF16),
            jax.ShapeDtypeStruct((544, 128), BF16),
            jax.ShapeDtypeStruct((1, 240), F32),
            jax.ShapeDtypeStruct((336, 128), F32),
        ],
        scratch_shapes=[pltpu.VMEM((800, 128), F32), pltpu.VMEM((800, 128), F32), pltpu.VMEM((3, 128), F32)],
        compiler_params=pltpu.CompilerParams(vmem_limit_bytes=VMEM_LIMIT),
        name="update",
    )(lengths, gw, cols, extra, params, row_state, col_state)


def body(tokens, upstream, gate_pre, up_pre, param_shards, shard_rows, row_state, col_state):
    quarter, wext = prep(shard_rows, param_shards)
    gw, cols, extra = main(tokens, upstream, gate_pre, up_pre, quarter, wext)
    new_params, direction, rows, new_cols = update(
        shard_rows, gw, cols, extra, param_shards, row_state.reshape(1, 240), col_state.reshape(336, 128)
    )
    return (new_params, direction, rows.reshape(-1), new_cols.reshape(-1))


def solution(mesh):
    in_specs = (
        P(("rep", "dp"), None),
        P(("rep", "dp"), None),
        P(("rep", "dp"), None),
        P(("rep", "dp"), None),
        P("dp", None),
        P(),
        P(),
        P(),
    )
    out_specs = (P("dp", None), P("dp", None), P(), P())
    return jax.shard_map(body, mesh=mesh, in_specs=in_specs, out_specs=out_specs, check_vma=False)
```
